32 devices in a mesh: fsdp: 4 (over y, x), ctx: 8 (over z, core).
Axes of the slice: x: 2, y: 2, z: 4, core: 2. Of those that a mesh axis runs over, the one named last changes fastest.
Arguments:
- block_in: bfloat16 [4, 1024, 1536], P('fsdp', 'ctx'), may hold values from -6 to 6
- cotangent: bfloat16 [4, 1024, 1536], P('fsdp', 'ctx'), may hold values from -6 to 6
- positions: int32 [4, 1024], P('fsdp', 'ctx'), may hold values from 0 to 1023, as said below
- attend_weight: float32 [2, 1536, 3072], P(None, 'fsdp', 'ctx'), may hold values from -0.15625 to 0.15625
- attend_moment: float32 [2, 1536, 3072], P(None, 'fsdp', 'ctx'), as said below
- attend_variance: float32 [2, 1536, 3072], P(None, 'fsdp', 'ctx'), as said below
- output_weight: float32 [2, 1536, 1536], P(None, 'fsdp', 'ctx'), may hold values from -0.625 to 0.625
- output_moment: float32 [2, 1536, 1536], P(None, 'fsdp', 'ctx'), as said below
- output_variance: float32 [2, 1536, 1536], P(None, 'fsdp', 'ctx'), as said below
- expand_weight: float32 [2, 1536, 8192], P(None, 'fsdp', 'ctx'), may hold values from -0.15625 to 0.15625
- expand_moment: float32 [2, 1536, 8192], P(None, 'fsdp', 'ctx'), as said below
- expand_variance: float32 [2, 1536, 8192], P(None, 'fsdp', 'ctx'), as said below
- reduce_weight: float32 [2, 4096, 1536], P(None, 'fsdp', 'ctx'), may hold values from -0.09375 to 0.09375
- reduce_moment: float32 [2, 4096, 1536], P(None, 'fsdp', 'ctx'), as said below
- reduce_variance: float32 [2, 4096, 1536], P(None, 'fsdp', 'ctx'), as said below
- gains: float32 [4, 1536], P(None, ('fsdp', 'ctx')), may hold values from 0.5 to 1.5
- gains_moment: float32 [4, 1536], P(None, ('fsdp', 'ctx')), as said below
- gains_variance: float32 [4, 1536], P(None, ('fsdp', 'ctx')), as said below
Outputs:
- block_out: float32 [4, 1024, 1536], P('fsdp', 'ctx')
- input_grad: float32 [4, 1024, 1536], P('fsdp', 'ctx')
- renewed_attend: float32 [2, 1536, 3072], P(None, 'fsdp', 'ctx')
- moment_attend: float32 [2, 1536, 3072], P(None, 'fsdp', 'ctx')
- variance_attend: float32 [2, 1536, 3072], P(None, 'fsdp', 'ctx')
- renewed_output: float32 [2, 1536, 1536], P(None, 'fsdp', 'ctx')
- moment_output: float32 [2, 1536, 1536], P(None, 'fsdp', 'ctx')
- variance_output: float32 [2, 1536, 1536], P(None, 'fsdp', 'ctx')
- renewed_expand: float32 [2, 1536, 8192], P(None, 'fsdp', 'ctx')
- moment_expand: float32 [2, 1536, 8192], P(None, 'fsdp', 'ctx')
- variance_expand: float32 [2, 1536, 8192], P(None, 'fsdp', 'ctx')
- renewed_reduce: float32 [2, 4096, 1536], P(None, 'fsdp', 'ctx')
- moment_reduce: float32 [2, 4096, 1536], P(None, 'fsdp', 'ctx')
- variance_reduce: float32 [2, 4096, 1536], P(None, 'fsdp', 'ctx')
- renewed_gains: float32 [4, 1536], P(None, ('fsdp', 'ctx'))
- moment_gains: float32 [4, 1536], P(None, ('fsdp', 'ctx'))
- variance_gains: float32 [4, 1536], P(None, ('fsdp', 'ctx'))
The draws below stay inside these ranges and needn't reach their ends.
Inputs may be any that keep to these rules, and one draw needn't show every extreme that they name: Each row of positions arranges 0 to 1023 in runs of 64 rising consecutive positions, each run starting at a multiple of 64; which run lies where is drawn for each sequence. `attend_moment`: about a ninth of the typical gradient entry of its parameter times the square root of the tokens summed, both signs. `attend_variance`: Positive, about 0.03 to 0.4 times the square of the typical gradient entry. `output_moment`: as attend_moment, for output_weight. `output_variance`: as attend_variance, for output_weight. `expand_moment`: as attend_moment, for expand_weight. `expand_variance`: as attend_variance, for expand_weight. `reduce_moment`: as attend_moment, for reduce_weight. `reduce_variance`: as attend_variance, for reduce_weight. `gains_moment`: as attend_moment, for the gains. `gains_variance`: as attend_variance, for the gains.
All inputs are finite; a program needn't handle non-finite values.
Results may differ from the reference program's by a relative error of at most 0.033.
Values may be sent and summed in bfloat16 or wider, within the bound.
No kernel may reach another device: no remote copies, remote signals or barrier semaphores. Data moves between devices by JAX's collectives and lax.ppermute only.
A program may use at most 384 MiB of HBM per device.

```python
import math
import jax
import jax.numpy as jnp
from jax import lax

D = 1536
HEADS = 16
KV_HEADS = 8
HEAD = 96
FF = 4096
LAYERS = 2
STEP = 10
TOK_DEV = 128
SEQS = 4
LENGTH = 1024
QKV = 3072


def grad_scale(factor):
    return factor * math.sqrt(SEQS * LENGTH)


def moment_draw(key, shape, factor):
    return grad_scale(factor) / 9.0 * jax.random.normal(key, shape, jnp.float32)


def variance_draw(key, shape, factor):
    spread = jax.random.uniform(key, shape, jnp.float32, math.log(0.5), math.log(8.0))
    return 0.05 / 0.95 * grad_scale(factor) ** 2 * jnp.exp(spread)


def draw_positions(key, part):
    key = jax.random.fold_in(key, 21)
    pieces = 2 * LENGTH // TOK_DEV
    half = TOK_DEV // 2
    seq_keys = jax.random.split(key, SEQS)

    def arrange(single):
        return jax.random.permutation(single, pieces).astype(jnp.int32)
    orders = jax.vmap(arrange)(seq_keys)
    within = jnp.arange(half, dtype=jnp.int32)
    return (orders[:, :, None] * half + within[None, None, :]).reshape(SEQS, LENGTH)


def draw_attend_moment(key, part):
    key = jax.random.fold_in(key, 11)
    return moment_draw(key, (LAYERS, D, D + 2 * KV_HEADS * HEAD), 0.3)


def draw_attend_variance(key, part):
    key = jax.random.fold_in(key, 12)
    return variance_draw(key, (LAYERS, D, D + 2 * KV_HEADS * HEAD), 0.3)


def draw_output_moment(key, part):
    key = jax.random.fold_in(key, 13)
    return moment_draw(key, (LAYERS, D, D), 0.2)


def draw_output_variance(key, part):
    key = jax.random.fold_in(key, 14)
    return variance_draw(key, (LAYERS, D, D), 0.2)


def draw_expand_moment(key, part):
    key = jax.random.fold_in(key, 15)
    return moment_draw(key, (LAYERS, D, 2 * FF), 0.35)


def draw_expand_variance(key, part):
    key = jax.random.fold_in(key, 16)
    return variance_draw(key, (LAYERS, D, 2 * FF), 0.35)


def draw_reduce_moment(key, part):
    key = jax.random.fold_in(key, 17)
    return moment_draw(key, (LAYERS, FF, D), 0.6)


def draw_reduce_variance(key, part):
    key = jax.random.fold_in(key, 18)
    return variance_draw(key, (LAYERS, FF, D), 0.6)


def draw_gains_moment(key, part):
    key = jax.random.fold_in(key, 19)
    return moment_draw(key, (2 * LAYERS, D), 0.5)


def draw_gains_variance(key, part):
    key = jax.random.fold_in(key, 20)
    return variance_draw(key, (2 * LAYERS, D), 0.5)


def block_levels(own_key, extent, cuts, smallest, top_value):
    loudness, own = 1.0, jax.random.fold_in(own_key, 6)
    for dim, blocks in cuts:
        heights = jnp.exp(jax.random.uniform(jax.random.fold_in(own, dim), (blocks,), jnp.float32, smallest / len(cuts), top_value / len(cuts)))
        loudness = loudness * jnp.repeat(heights, extent[dim] // blocks).reshape([-1 if axis == dim else 1 for axis in range(len(extent))])
    return loudness


def gaussian(stream_key, dims, scale, limit, shards=(), kind=jnp.bfloat16):
    values = jax.random.normal(stream_key, dims, jnp.float32) * scale
    if len(shards) > 0:
        values = block_levels(stream_key, dims, shards, -0.22, 0.18) * values
    return jnp.clip(values, min=-limit, max=limit).astype(kind)


def setup_inputs(seed: int = 0) -> dict:
    arg_keys = jax.random.split(jax.random.key(seed), 19)
    return {
        "block_in": gaussian(arg_keys[0], (SEQS, LENGTH, D), 1.0, 6.0, ((0, 4), (1, 8))),
        "cotangent": gaussian(arg_keys[1], (SEQS, LENGTH, D), 1.0, 6.0, ((0, 4), (1, 8))),
        "positions": draw_positions(jax.random.fold_in(arg_keys[18], 71), 0),
        "attend_weight": gaussian(arg_keys[3], (LAYERS, D, QKV), D ** -0.5, 0.15625, ((1, 4), (2, 8)), jnp.float32),
        "attend_moment": draw_attend_moment(jax.random.fold_in(arg_keys[18], 71), 0),
        "attend_variance": draw_attend_variance(jax.random.fold_in(arg_keys[18], 71), 0),
        "output_weight": gaussian(arg_keys[6], (LAYERS, D, D), (D // 16) ** -0.5, 0.625, ((1, 4), (2, 8)), jnp.float32),
        "output_moment": draw_output_moment(jax.random.fold_in(arg_keys[18], 71), 0),
        "output_variance": draw_output_variance(jax.random.fold_in(arg_keys[18], 71), 0),
        "expand_weight": gaussian(arg_keys[9], (LAYERS, D, 2 * FF), D ** -0.5, 0.15625, ((1, 4), (2, 8)), jnp.float32),
        "expand_moment": draw_expand_moment(jax.random.fold_in(arg_keys[18], 71), 0),
        "expand_variance": draw_expand_variance(jax.random.fold_in(arg_keys[18], 71), 0),
        "reduce_weight": gaussian(arg_keys[12], (LAYERS, FF, D), FF ** -0.5, 0.09375, ((1, 4), (2, 8)), jnp.float32),
        "reduce_moment": draw_reduce_moment(jax.random.fold_in(arg_keys[18], 71), 0),
        "reduce_variance": draw_reduce_variance(jax.random.fold_in(arg_keys[18], 71), 0),
        "gains": jnp.clip(1.0 + 0.1 * jax.random.normal(arg_keys[15], (2 * LAYERS, D), jnp.float32), 0.5, 1.5),
        "gains_moment": draw_gains_moment(jax.random.fold_in(arg_keys[18], 71), 0),
        "gains_variance": draw_gains_variance(jax.random.fold_in(arg_keys[18], 71), 0),
    }


EPS = 1e-05
THETA = 100000.0
DECAY_FIRST = 0.9
DECAY_SECOND = 0.95
ADAM_EPS = 1e-08
WEIGHT_DECAY = 0.1
RATE_MATRIX = 0.06
RATE_GAIN = 0.6

@jax.custom_vjp
def low(v):
    return lax.optimization_barrier(v.astype(jnp.bfloat16)).astype(jnp.float32)

@jax.custom_vjp
def low_back(v):
    return v

def low_keep(v):
    return (low(v), None)

def low_pass(kept, grad):
    return (grad,)

def back_keep(v):
    return (v, None)

def back_low(kept, grad):
    return (low(grad),)
low.defvjp(low_keep, low_pass)
low_back.defvjp(back_keep, back_low)

def matmul(left, right):
    return jnp.dot(left, right, precision=lax.Precision.HIGHEST, preferred_element_type=jnp.float32)

def rms_norm(stream, gain):
    return stream * lax.rsqrt(lax.optimization_barrier(jnp.mean(stream * stream, axis=-1, keepdims=True)) + EPS) * gain

def rotate(tensor, order):
    half = HEAD // 2
    freq = THETA ** (-2.0 * jnp.arange(half, dtype=jnp.float32) / HEAD)
    angle = order.astype(jnp.float32)[:, None] * freq[None, :]
    cosine = jnp.cos(angle)[:, None, :]
    sine = jnp.sin(angle)[:, None, :]
    first = tensor[..., :half]
    second = tensor[..., half:]
    return jnp.concatenate([first * cosine - second * sine, second * cosine + first * sine], axis=-1)

def attention(queries, keys_rot, values, order):
    group = HEADS // KV_HEADS
    scale = 1.0 / math.sqrt(HEAD)
    rows = 2 * TOK_DEV if LENGTH % (2 * TOK_DEV) == 0 else TOK_DEV
    count = LENGTH // rows
    query_blocks = queries.reshape(count, rows, KV_HEADS, group, HEAD)
    order_blocks = order.reshape(count, rows)

    def one_block(inputs):
        query_block, order_block = inputs
        scores = jnp.einsum('rgeh,kgh->gerk', query_block, keys_rot, precision=lax.Precision.HIGHEST) * scale
        scores = low_back(scores)
        allowed = (order[None, :] <= order_block[:, None])[None, None]
        masked = jnp.where(allowed, scores, -1e+30)
        top = lax.optimization_barrier(jnp.max(masked, axis=-1, keepdims=True))
        expos = jnp.where(allowed, jnp.exp(masked - top), 0.0)
        probs = expos / lax.optimization_barrier(jnp.sum(expos, axis=-1, keepdims=True))
        return jnp.einsum('gerk,kgh->rgeh', low(probs), values, precision=lax.Precision.HIGHEST)
    mixed = lax.map(jax.checkpoint(one_block), (query_blocks, order_blocks))
    return mixed.reshape(LENGTH, HEADS * HEAD)

def layer(stream, order, attend_rows, output_rows, expand_rows, reduce_rows, gain_attend, gain_mix):
    kv_width = KV_HEADS * HEAD
    normed = low(rms_norm(stream, gain_attend))
    projected = low_back(matmul(normed, attend_rows))
    queries = low_back(low(rotate(projected[:, :D].reshape(LENGTH, HEADS, HEAD), order)))
    keys_rot = low_back(low(rotate(projected[:, D:D + kv_width].reshape(LENGTH, KV_HEADS, HEAD), order)))
    values = low(projected[:, D + kv_width:].reshape(LENGTH, KV_HEADS, HEAD))
    mixed = low_back(low(attention(queries, keys_rot, values, order)))
    stream = stream + low_back(matmul(mixed, output_rows))
    normed_mid = low(rms_norm(stream, gain_mix))
    gate_up = low_back(matmul(normed_mid, expand_rows))
    hidden = low(jax.nn.silu(gate_up[:, :FF]) * gate_up[:, FF:])
    return stream + low_back(matmul(hidden, reduce_rows))

def adamw(weight, moment, variance, grad, rate, decay):
    moment = DECAY_FIRST * moment + (1.0 - DECAY_FIRST) * grad
    variance = DECAY_SECOND * variance + (1.0 - DECAY_SECOND) * grad * grad
    update = moment / (1.0 - DECAY_FIRST ** STEP) / (jnp.sqrt(variance / (1.0 - DECAY_SECOND ** STEP)) + ADAM_EPS)
    return (weight - rate * (update + decay * weight), moment, variance)

def reference(block_in, cotangent, positions, attend_weight, attend_moment, attend_variance, output_weight, output_moment, output_variance, expand_weight, expand_moment, expand_variance, reduce_weight, reduce_moment, reduce_variance, gains, gains_moment, gains_variance):
    masters = (attend_weight, output_weight, expand_weight, reduce_weight)
    rounded = tuple((master.astype(jnp.bfloat16).astype(jnp.float32) for master in masters))

    def forward(stream, order, weights, gain_table):
        for layer_index in range(LAYERS):
            stream = layer(stream, order, weights[0][layer_index], weights[1][layer_index], weights[2][layer_index], weights[3][layer_index], gain_table[2 * layer_index], gain_table[2 * layer_index + 1])
        return stream

    def per_sequence(carry, inputs):
        seq_in, seq_cot, seq_order = inputs

        def run(stream, weights, gain_table):
            return forward(stream, seq_order, weights, gain_table)
        result, pullback = jax.vjp(run, seq_in.astype(jnp.float32), rounded, gains)
        grad_in, grad_weights, grad_gains = pullback(seq_cot.astype(jnp.float32))
        summed = tuple((total + term for total, term in zip(carry[0], grad_weights)))
        return ((summed, carry[1] + grad_gains), (result, grad_in))
    start = (tuple((jnp.zeros_like(weight) for weight in rounded)), jnp.zeros_like(gains))
    (grad_weights, grad_gains), (block_out, input_grad) = lax.scan(per_sequence, start, (block_in, cotangent, positions))
    renewed = []
    for master, moment, variance, grad in zip(masters, (attend_moment, output_moment, expand_moment, reduce_moment), (attend_variance, output_variance, expand_variance, reduce_variance), grad_weights):
        renewed.append(adamw(master, moment, variance, grad, RATE_MATRIX, WEIGHT_DECAY))
    gain_state = adamw(gains, gains_moment, gains_variance, grad_gains, RATE_GAIN, 0.0)
    return (block_out, input_grad, renewed[0][0], renewed[0][1], renewed[0][2], renewed[1][0], renewed[1][1], renewed[1][2], renewed[2][0], renewed[2][1], renewed[2][2], renewed[3][0], renewed[3][1], renewed[3][2], gain_state[0], gain_state[1], gain_state[2])
```

```python
import functools
import math

import jax
import jax.numpy as jnp
from jax import lax
from jax.experimental import pallas as pl
from jax.experimental.pallas import tpu as pltpu
from jax.sharding import PartitionSpec as P

HEADS = 16
KV_HEADS = 8
HEAD = 96
LAYERS = 2
STEP = 10

EPS = 1e-05
THETA = 100000.0
DECAY_FIRST = 0.9
DECAY_SECOND = 0.95
ADAM_EPS = 1e-08
WEIGHT_DECAY = 0.1
RATE_MATRIX = 0.06
RATE_GAIN = 0.6

BF16 = jnp.bfloat16
F32 = jnp.float32
SCALE = 1.0 / math.sqrt(HEAD)
GAIN_PARTS = 3
GAIN_ROWS = 16
BOTH = ("fsdp", "ctx")


def dot(left, right, contract_left, contract_right):
    return lax.dot_general(
        left,
        right,
        (((contract_left,), (contract_right,)), ((), ())),
        preferred_element_type=F32,
    )


def swap(value, distance, size):
    return lax.ppermute(value, "fsdp", [(i, i ^ distance) for i in range(size)])


def swap_core(value, cycle):
    return lax.ppermute(value, "ctx", [(i, i ^ 1) for i in range(cycle)])


def sequence_pairs(size, cycle):
    return [
        (f * cycle + 2 * z + core, z * cycle + 2 * f + core)
        for f in range(size)
        for z in range(size)
        for core in range(2)
    ]


def block_pairs(size, cycle):
    return [
        (f * cycle + u * size + r, r * cycle + u * size + f)
        for f in range(size)
        for u in range(2)
        for r in range(size)
    ]


def attend_pairs(size, cycle):
    both = []
    for odd in range(2):
        pairs = []
        for row in range(size):
            for f in range(size):
                pairs.append((row * cycle + f, f * cycle + row))
            for k in range(size // 2):
                key_to, value_to = (2 * k + odd, 2 * k + 1 - odd)
                pairs.append((row * cycle + size + k, key_to * cycle + size + row))
                pairs.append((row * cycle + size + size // 2 + k, value_to * cycle + size + row))
        both.append(pairs)
    return both


def backwards(pairs):
    return [(target, source) for source, target in pairs]


def exchange_attend(first, second, flip_here, flip_there, pairs_first, pairs_second):
    lead = jnp.where(flip_here, second, first)
    tail = jnp.where(flip_here, first, second)
    lead = lax.ppermute(lead, BOTH, pairs_first)
    tail = lax.ppermute(tail, BOTH, pairs_second)
    return jnp.where(flip_there, tail, lead), jnp.where(flip_there, lead, tail)


def gather_tokens(piece, size):
    if size != 4:
        return jnp.concatenate([piece] + [swap(piece, k, size) for k in range(1, size)])
    half = piece.shape[0] // 2
    one = swap(piece, 1, size)
    two = swap(piece, 2, size)
    three_top = swap(one[:half], 2, size)
    three_low = swap(two[half:], 1, size)
    return jnp.concatenate([piece, one, two, three_top, three_low])


def scatter_tokens(partial, size):
    tokens = partial.shape[0] // size
    chunks = [partial[k * tokens : (k + 1) * tokens] for k in range(size)]
    if size != 4:
        total = chunks[0]
        for k in range(1, size):
            total = total + swap(chunks[k].astype(BF16), k, size).astype(F32)
        return total
    half = tokens // 2
    far = chunks[3].astype(BF16)
    via_one = swap(far[:half], 1, size).astype(F32)
    via_two = swap(far[half:], 2, size).astype(F32)
    one = jnp.concatenate([chunks[1][:half], chunks[1][half:] + via_two]).astype(BF16)
    two = jnp.concatenate([chunks[2][:half] + via_one, chunks[2][half:]]).astype(BF16)
    return chunks[0] + swap(one, 1, size).astype(F32) + swap(two, 2, size).astype(F32)


def attend_kernel(query, keys_own, keys_far, value_own, value_far, order, order_own, order_far, out, totals):
    queries = query[...]
    here = order[...]

    def scores(keys, key_order):
        block = dot(keys[...].T, queries, 1, 0) * SCALE
        return jnp.where(key_order[...] <= here, block, -1e30)

    own = scores(keys_own, order_own)
    far = scores(keys_far, order_far)
    top = jnp.maximum(jnp.max(own, axis=0, keepdims=True), jnp.max(far, axis=0, keepdims=True))
    own = jnp.exp(own - top)
    far = jnp.exp(far - top)
    total = jnp.sum(own, axis=0, keepdims=True) + jnp.sum(far, axis=0, keepdims=True)
    mixed = dot(value_own[...], own.astype(BF16), 1, 0) + dot(value_far[...], far.astype(BF16), 1, 0)
    out[...] = (mixed / total).astype(BF16)
    totals[0] = top + jnp.log(total)


def attend(queries, pair_own, pair_far, order, order_far):
    width, tokens = queries.shape
    kv_heads = pair_own.shape[0] // (2 * HEAD)
    group = width // HEAD // kv_heads
    head = lambda g, e: (g * group + e, 0)
    key = lambda g, e: (g, 0)
    value = lambda g, e: (kv_heads + g, 0)
    whole = lambda g, e: (0, 0)
    kv_block = (HEAD, tokens)
    return pl.pallas_call(
        attend_kernel,
        grid=(kv_heads, group),
        in_specs=[
            pl.BlockSpec((HEAD, tokens), head),
            pl.BlockSpec(kv_block, key),
            pl.BlockSpec(kv_block, key),
            pl.BlockSpec(kv_block, value),
            pl.BlockSpec(kv_block, value),
            pl.BlockSpec((1, tokens), whole),
            pl.BlockSpec((tokens, 1), whole),
            pl.BlockSpec((tokens, 1), whole),
        ],
        out_specs=[
            pl.BlockSpec((HEAD, tokens), head),
            pl.BlockSpec((1, 1, tokens), lambda g, e: (g * group + e, 0, 0)),
        ],
        out_shape=[
            jax.ShapeDtypeStruct((width, tokens), BF16),
            jax.ShapeDtypeStruct((width // HEAD, 1, tokens), F32),
        ],
        compiler_params=pltpu.CompilerParams(vmem_limit_bytes=56 * 1024 * 1024),
        cost_estimate=pl.CostEstimate(
            flops=8 * width * tokens * tokens,
            bytes_accessed=12 * width * tokens,
            transcendentals=2 * tokens * tokens * width // HEAD,
        ),
        name="attend",
    )(queries, pair_own, pair_far, pair_own, pair_far, order[None, :], order[:, None], order_far[:, None])


def attend_back_kernel(
    query, grad, keys_own, keys_far, value_own, value_far, order, order_own, order_far, totals,
    grad_query, grad_own, grad_far, grad_value_own, grad_value_far,
):
    queries = query[...]
    grads = grad[...]
    here = order[...]
    first = pl.program_id(1) == 0

    def terms(keys, values, key_order):
        block = dot(keys[...].T, queries, 1, 0) * SCALE
        block = jnp.where(key_order[...] <= here, block, -1e30)
        probs = jnp.exp(block - totals[0])
        return probs, dot(values[...].T, grads, 1, 0)

    probs_own, back_own = terms(keys_own, value_own, order_own)
    probs_far, back_far = terms(keys_far, value_far, order_far)
    delta = jnp.sum(probs_own * back_own, axis=0, keepdims=True) + jnp.sum(
        probs_far * back_far, axis=0, keepdims=True
    )
    score_own = (probs_own * (back_own - delta)).astype(BF16)
    score_far = (probs_far * (back_far - delta)).astype(BF16)
    grad_query[...] = (
        dot(keys_own[...], score_own, 1, 0) + dot(keys_far[...], score_far, 1, 0)
    ) * SCALE
    results = (
        (grad_own, dot(queries, score_own, 1, 1) * SCALE),
        (grad_far, dot(queries, score_far, 1, 1) * SCALE),
        (grad_value_own, dot(grads, probs_own.astype(BF16), 1, 1)),
        (grad_value_far, dot(grads, probs_far.astype(BF16), 1, 1)),
    )

    @pl.when(first)
    def _():
        for ref, value in results:
            ref[...] = value

    @pl.when(jnp.logical_not(first))
    def _():
        for ref, value in results:
            ref[...] += value


def attend_back(queries, grads, pair_own, pair_far, order, order_far, totals):
    width, tokens = queries.shape
    kv_heads = pair_own.shape[0] // (2 * HEAD)
    group = width // HEAD // kv_heads
    head = lambda g, e: (g * group + e, 0)
    key = lambda g, e: (g, 0)
    value = lambda g, e: (kv_heads + g, 0)
    whole = lambda g, e: (0, 0)
    block = (HEAD, tokens)
    kv_shape = jax.ShapeDtypeStruct((kv_heads * HEAD, tokens), F32)
    return pl.pallas_call(
        attend_back_kernel,
        grid=(kv_heads, group),
        in_specs=[
            pl.BlockSpec(block, head),
            pl.BlockSpec(block, head),
            pl.BlockSpec(block, key),
            pl.BlockSpec(block, key),
            pl.BlockSpec(block, value),
            pl.BlockSpec(block, value),
            pl.BlockSpec((1, tokens), whole),
            pl.BlockSpec((tokens, 1), whole),
            pl.BlockSpec((tokens, 1), whole),
            pl.BlockSpec((1, 1, tokens), lambda g, e: (g * group + e, 0, 0)),
        ],
        out_specs=[
            pl.BlockSpec(block, head),
            pl.BlockSpec(block, key),
            pl.BlockSpec(block, key),
            pl.BlockSpec(block, key),
            pl.BlockSpec(block, key),
        ],
        out_shape=[jax.ShapeDtypeStruct((width, tokens), F32)] + [kv_shape] * 4,
        compiler_params=pltpu.CompilerParams(vmem_limit_bytes=60 * 1024 * 1024),
        cost_estimate=pl.CostEstimate(
            flops=20 * width * tokens * tokens,
            bytes_accessed=24 * width * tokens,
            transcendentals=2 * tokens * tokens * width // HEAD,
        ),
        name="attend_back",
    )(
        queries, grads, pair_own, pair_far, pair_own, pair_far,
        order[None, :], order[:, None], order_far[:, None], totals,
    )


def rotate(tensor, cosine, sine):
    half = HEAD // 2
    tokens = tensor.shape[1]
    split = tensor.reshape(-1, 2, half, tokens)
    first, second = (split[:, 0], split[:, 1])
    return jnp.stack(
        [first * cosine - second * sine, second * cosine + first * sine], axis=1
    ).reshape(-1, tokens)


def inverse_rms(stream):
    return lax.rsqrt(jnp.mean(stream * stream, axis=-1, keepdims=True) + EPS)


def norm_back(stream, gain, grad):
    scale = inverse_rms(stream)
    inner = jnp.mean(stream * gain * grad, axis=-1, keepdims=True)
    grad_stream = scale * (gain * grad) - stream * (scale * scale * scale * inner)
    return grad_stream, jnp.sum(grad * stream * scale, axis=0)


def adamw(weight, moment, variance, grad, rate, decay):
    moment = DECAY_FIRST * moment + (1.0 - DECAY_FIRST) * grad
    variance = DECAY_SECOND * variance + (1.0 - DECAY_SECOND) * grad * grad
    update = (
        moment
        / (1.0 - DECAY_FIRST**STEP)
        / (jnp.sqrt(variance / (1.0 - DECAY_SECOND**STEP)) + ADAM_EPS)
    )
    return (weight - rate * (update + decay * weight), moment, variance)


def body(
    block_in,
    cotangent,
    positions,
    attend_weight,
    attend_moment,
    attend_variance,
    output_weight,
    output_moment,
    output_variance,
    expand_weight,
    expand_moment,
    expand_variance,
    reduce_weight,
    reduce_moment,
    reduce_variance,
    gains,
    gains_moment,
    gains_variance,
):
    size = lax.axis_size("fsdp")
    cycle = lax.axis_size("ctx")
    row = lax.axis_index("fsdp")
    column = lax.axis_index("ctx")
    model = block_in.shape[2]
    att_rows, att_cols = attend_weight.shape[1:]
    out_rows, out_cols = output_weight.shape[1:]
    exp_rows, exp_cols = expand_weight.shape[1:]
    red_rows, red_cols = reduce_weight.shape[1:]
    gain_cols = gains.shape[1]
    by_sequence = sequence_pairs(size, cycle)
    by_block = block_pairs(size, cycle)
    by_half = attend_pairs(size, cycle)
    holds_values = column >= size + size // 2
    mixed_up = jnp.logical_and(column >= size, row % 2 == 1)
    half = att_cols // 2
    others = jnp.bitwise_xor(row, jnp.arange(size))

    def send_attend(layer):
        low = attend_weight[layer].astype(BF16)
        lead, tail = exchange_attend(
            low[:, :half], low[:, half:], holds_values, mixed_up, by_half[0], by_half[1]
        )
        return jnp.concatenate([lead, tail], axis=1)

    def gather(parts):
        return lax.all_gather(jnp.concatenate(parts), "ctx", axis=0, tiled=False)

    pieces = []
    rest = gains
    for _ in range(GAIN_PARTS):
        part = rest.astype(BF16)
        rest = rest - part.astype(F32)
        pieces.append(part)
    gain_own = jnp.stack(pieces)
    gain_all = jnp.stack([gain_own] + [swap(gain_own, k, size) for k in range(1, size)])
    gain_all = jnp.take(gain_all, others, axis=0)
    gain_flat = gain_all.reshape(-1, att_cols)
    gain_used = gain_flat.shape[0]
    gain_pad = jnp.zeros((GAIN_ROWS - gain_used, att_cols), BF16)

    attn_parts = []
    mlp_parts = []
    for layer in range(LAYERS):
        attn = [send_attend(layer), output_weight[layer].astype(BF16).T]
        if layer == 0:
            attn += [gain_flat, gain_pad]
        attn_parts.append(gather(attn))
        mlp_parts.append(
            gather(
                [
                    lax.ppermute(expand_weight[layer].astype(BF16), BOTH, by_block),
                    reduce_weight[layer].astype(BF16).T,
                ]
            )
        )

    gain_table = attn_parts[0][:, att_rows + out_cols : att_rows + out_cols + gain_used]
    gain_table = gain_table.reshape(cycle, size, GAIN_PARTS, 2 * LAYERS, gain_cols).astype(F32)
    gain_table = gain_table[:, :, 0] + gain_table[:, :, 1] + gain_table[:, :, 2]
    gain_table = jnp.transpose(gain_table, (2, 1, 0, 3)).reshape(2 * LAYERS, model)

    def attn_weights(layer):
        part = attn_parts[layer]
        block = part[:, :att_rows]
        return (
            block[:size].reshape(model, att_cols),
            block[size:].reshape(model, att_cols),
            part[:, att_rows : att_rows + out_cols].reshape(model, out_rows),
        )

    def mlp_weights(layer):
        part = mlp_parts[layer]
        block = part[:, :exp_rows]
        return (
            block[:size].reshape(model, exp_cols),
            block[size:].reshape(model, exp_cols),
            part[:, exp_rows:].reshape(model, red_rows),
        )

    stream_low = lax.ppermute(block_in[0], BOTH, by_sequence)
    back_low = lax.ppermute(cotangent[0], BOTH, by_sequence)
    order = gather_tokens(lax.ppermute(positions[0], BOTH, by_sequence), size)
    order_far = swap_core(order, cycle)
    freq = THETA ** (-2.0 * jnp.arange(HEAD // 2, dtype=F32) / HEAD)
    angle = freq[:, None] * order.astype(F32)[None, :]
    cosine, sine = (jnp.cos(angle), jnp.sin(angle))

    stream = stream_low.astype(F32)
    stream_first = gather_tokens(stream_low, size).astype(F32)
    saved = []
    for layer in range(LAYERS):
        gain_attend, gain_mix = (gain_table[2 * layer], gain_table[2 * layer + 1])
        query_weight, pair_weight, output_t = attn_weights(layer)
        if layer == 0:
            acts = (stream_first * inverse_rms(stream_first) * gain_attend).astype(BF16)
        else:
            acts = gather_tokens((stream * inverse_rms(stream) * gain_attend).astype(BF16), size)
        queries = rotate(dot(query_weight, acts, 0, 1), cosine, sine).astype(BF16)
        pair = dot(pair_weight, acts, 0, 1)
        pair = jnp.concatenate(
            [rotate(pair[: pair.shape[0] // 2], cosine, sine), pair[pair.shape[0] // 2 :]]
        ).astype(BF16)
        pair_far = swap_core(pair, cycle)
        mixed, totals = attend(queries, pair, pair_far, order, order_far)
        middle = stream + scatter_tokens(dot(mixed, output_t, 0, 1), size)
        gate_weight, up_weight, reduce_t = mlp_weights(layer)
        middle_low = gather_tokens((middle * inverse_rms(middle) * gain_mix).astype(BF16), size)
        gate = dot(middle_low, gate_weight, 1, 0)
        up = dot(middle_low, up_weight, 1, 0)
        hidden = (jax.nn.silu(gate) * up).astype(BF16)
        stream_next = middle + scatter_tokens(dot(hidden, reduce_t, 1, 1), size)
        saved.append((stream, acts, queries, pair, pair_far, mixed, totals, middle, middle_low, gate, up, hidden))
        stream = stream_next
    block_out = lax.ppermute(stream, BOTH, by_sequence)

    back = back_low.astype(F32)
    back_all = gather_tokens(back_low, size)
    grads = {}
    gain_grads = [None] * (2 * LAYERS)

    def reduce(parts):
        return lax.psum_scatter(
            jnp.concatenate(parts, axis=1), "ctx", scatter_dimension=0, tiled=False
        ).astype(F32)

    for layer in reversed(range(LAYERS)):
        stream, acts, queries, pair, pair_far, mixed, totals, middle, middle_low, gate, up, hidden = saved[layer]
        gain_attend, gain_mix = (gain_table[2 * layer], gain_table[2 * layer + 1])
        query_weight, pair_weight, output_t = attn_weights(layer)
        gate_weight, up_weight, reduce_t = mlp_weights(layer)
        if layer < LAYERS - 1:
            back_all = gather_tokens(back.astype(BF16), size)
        grad_hidden = dot(back_all, reduce_t, 1, 0)
        sigmoid = jax.nn.sigmoid(gate)
        grad_gate = (grad_hidden * up * (sigmoid * (1.0 + gate * (1.0 - sigmoid)))).astype(BF16)
        grad_up = (grad_hidden * (gate * sigmoid)).astype(BF16)
        grad_middle = scatter_tokens(
            dot(grad_gate, gate_weight, 1, 1) + dot(grad_up, up_weight, 1, 1), size
        )
        mlp_grad = reduce(
            [
                jnp.concatenate(
                    [dot(middle_low, grad_gate, 0, 0), dot(middle_low, grad_up, 0, 0)]
                )
                .astype(BF16)
                .reshape(cycle, exp_rows, exp_cols),
                dot(back_all, hidden, 0, 0).astype(BF16).reshape(cycle, red_cols, red_rows),
            ]
        )
        grads["expand", layer] = lax.ppermute(
            mlp_grad[:exp_rows].astype(BF16), BOTH, backwards(by_block)
        ).astype(F32)
        grads["reduce", layer] = mlp_grad[exp_rows:].T
        change, gain_grads[2 * layer + 1] = norm_back(middle, gain_mix, grad_middle)
        back = back + change
        back_attend = gather_tokens(back.astype(BF16), size)
        grad_mixed = dot(output_t, back_attend, 0, 1).astype(BF16)
        grad_query, key_own, key_far, value_own, value_far = attend_back(
            queries, grad_mixed, pair, pair_far, order, order_far, totals
        )
        from_far = swap_core(jnp.concatenate([key_far, value_far]).astype(BF16), cycle).astype(F32)
        rows_kv = key_own.shape[0]
        grad_key = key_own + from_far[:rows_kv]
        grad_value = value_own + from_far[rows_kv:]
        grad_query = rotate(grad_query.astype(BF16).astype(F32), cosine, -sine).astype(BF16)
        grad_key = rotate(grad_key.astype(BF16).astype(F32), cosine, -sine).astype(BF16)
        grad_pair = jnp.concatenate([grad_key, grad_value.astype(BF16)])
        grad_acts = dot(grad_query, query_weight, 0, 1) + dot(grad_pair, pair_weight, 0, 1)
        parts = [
            jnp.concatenate([dot(acts, grad_query, 0, 1), dot(acts, grad_pair, 0, 1)])
            .astype(BF16)
            .reshape(cycle, att_rows, att_cols),
            dot(back_attend, mixed, 0, 1).astype(BF16).reshape(cycle, out_cols, out_rows),
        ]
        grad_stream = scatter_tokens(grad_acts, size)
        change, gain_grads[2 * layer] = norm_back(stream, gain_attend, grad_stream)
        back = back + change
        if layer == 0:
            gain_grads[0] = jnp.sum(grad_acts * stream_first * inverse_rms(stream_first), axis=0)
            table = jnp.stack(gain_grads).reshape(2 * LAYERS, size, cycle, gain_cols)
            table = jnp.transpose(table, (2, 1, 0, 3)).astype(BF16).reshape(cycle, -1, att_cols)
            fill = jnp.zeros((cycle, GAIN_ROWS - table.shape[1], att_cols), BF16)
            parts += [table, fill]
        attn_grad = reduce(parts)
        block = attn_grad[:att_rows].astype(BF16)
        lead, tail = exchange_attend(
            block[:, :half],
            block[:, half:],
            mixed_up,
            holds_values,
            backwards(by_half[0]),
            backwards(by_half[1]),
        )
        grads["attend", layer] = jnp.concatenate([lead, tail], axis=1).astype(F32)
        grads["output", layer] = attn_grad[att_rows : att_rows + out_cols].T
        if layer == 0:
            grad_gains = attn_grad[att_rows + out_cols : att_rows + out_cols + table.shape[1]]
            grad_gains = grad_gains.reshape(size, 2 * LAYERS, gain_cols)
            grad_gains = jnp.take(grad_gains, others, axis=0)
            total = grad_gains[0]
            for k in range(1, size):
                total = total + swap(grad_gains[k], k, size)
            grad_gains = total
    input_grad = lax.ppermute(back, BOTH, by_sequence)

    results = []
    for name, state in (
        ("attend", (attend_weight, attend_moment, attend_variance)),
        ("output", (output_weight, output_moment, output_variance)),
        ("expand", (expand_weight, expand_moment, expand_variance)),
        ("reduce", (reduce_weight, reduce_moment, reduce_variance)),
    ):
        grad = jnp.stack([grads[name, layer] for layer in range(LAYERS)])
        results += list(adamw(*state, grad, RATE_MATRIX, WEIGHT_DECAY))
    results += list(adamw(gains, gains_moment, gains_variance, grad_gains, RATE_GAIN, 0.0))
    return (block_out[None], input_grad[None], *results)


def solution(mesh):
    tokens = P("fsdp", "ctx", None)
    matrix = P(None, "fsdp", "ctx")
    gain = P(None, ("fsdp", "ctx"))
    return jax.shard_map(
        body,
        mesh=mesh,
        in_specs=(tokens, tokens, P("fsdp", "ctx")) + (matrix,) * 12 + (gain,) * 3,
        out_specs=(tokens, tokens) + (matrix,) * 12 + (gain,) * 3,
        check_vma=False,
    )
```

```python
import functools
import math

import jax
import jax.numpy as jnp
from jax import lax
from jax.experimental import pallas as pl
from jax.experimental.pallas import tpu as pltpu
from jax.sharding import PartitionSpec as P

HEADS = 16
KV_HEADS = 8
HEAD = 96
LAYERS = 2
STEP = 10

EPS = 1e-05
THETA = 100000.0
DECAY_FIRST = 0.9
DECAY_SECOND = 0.95
ADAM_EPS = 1e-08
WEIGHT_DECAY = 0.1
RATE_MATRIX = 0.06
RATE_GAIN = 0.6

BF16 = jnp.bfloat16
F32 = jnp.float32
SCALE = 1.0 / math.sqrt(HEAD)
GAIN_PARTS = 3
GAIN_ROWS = 16
RUN = 64
LANES = 128
BOTH = ("fsdp", "ctx")
VMEM_LIMIT = 60 * 1024 * 1024


def dot(left, right, contract_left, contract_right):
    return lax.dot_general(
        left,
        right,
        (((contract_left,), (contract_right,)), ((), ())),
        preferred_element_type=F32,
    )


def after(value, *events):
    return lax.optimization_barrier((value, *events))[0]


def swap(value, distance, size):
    return lax.ppermute(value, "fsdp", [(i, i ^ distance) for i in range(size)])


def swap_core(value, cycle):
    return lax.ppermute(value, "ctx", [(i, i ^ 1) for i in range(cycle)])


def exchange(parts, axis, step, size):
    cycle = lax.axis_size(axis)
    received = [parts[0]]
    for k in range(1, size):
        received.append(lax.ppermute(parts[k], axis, [(i, i ^ (k * step)) for i in range(cycle)]))
    return jnp.stack(received)


def to_plane(value, size, row, plane):
    far = jnp.bitwise_xor(row, jnp.arange(size))
    parts = value.reshape(size, -1, value.shape[-1])
    parts = exchange(jnp.take(parts, far, axis=0), "fsdp", 1, size)
    parts = exchange(jnp.take(parts, jnp.bitwise_xor(far, plane), axis=0), "ctx", 2, size)
    return parts.reshape(value.shape)


def from_plane(value, size, row, plane):
    far = jnp.bitwise_xor(row, jnp.arange(size))
    parts = value.reshape(size, -1, value.shape[-1])
    parts = exchange(parts, "ctx", 2, size)
    parts = exchange(jnp.take(parts, jnp.bitwise_xor(far, plane), axis=0), "fsdp", 1, size)
    return jnp.take(parts, far, axis=0).reshape(value.shape)


def attend_pairs(size, cycle):
    both = []
    for odd in range(2):
        pairs = []
        for row in range(size):
            for f in range(size):
                pairs.append((row * cycle + f, f * cycle + row))
            for k in range(size // 2):
                key_to, value_to = (2 * k + odd, 2 * k + 1 - odd)
                pairs.append((row * cycle + size + k, key_to * cycle + size + row))
                pairs.append((row * cycle + size + size // 2 + k, value_to * cycle + size + row))
        both.append(pairs)
    return both


def backwards(pairs):
    return [(target, source) for source, target in pairs]


def exchange_attend(first, second, flip_here, flip_there, pairs_first, pairs_second):
    lead = jnp.where(flip_here, second, first)
    tail = jnp.where(flip_here, first, second)
    lead = lax.ppermute(lead, BOTH, pairs_first)
    tail = lax.ppermute(tail, BOTH, pairs_second)
    return jnp.where(flip_there, tail, lead), jnp.where(flip_there, lead, tail)


def gather_tokens(piece, size):
    if size != 4:
        return jnp.concatenate([piece] + [swap(piece, k, size) for k in range(1, size)])
    half = piece.shape[0] // 2
    one = swap(piece, 1, size)
    two = swap(piece, 2, size)
    three_top = swap(one[:half], 2, size)
    three_low = swap(two[half:], 1, size)
    return jnp.concatenate([piece, one, two, three_top, three_low])


def scatter_tokens(partial, size):
    tokens = partial.shape[0] // size
    chunks = [partial[k * tokens : (k + 1) * tokens].astype(F32) for k in range(size)]
    if size != 4:
        total = chunks[0]
        for k in range(1, size):
            total = total + swap(chunks[k].astype(BF16), k, size).astype(F32)
        return total
    half = tokens // 2
    far = chunks[3].astype(BF16)
    via_one = swap(far[:half], 1, size).astype(F32)
    via_two = swap(far[half:], 2, size).astype(F32)
    one = jnp.concatenate([chunks[1][:half], chunks[1][half:] + via_two]).astype(BF16)
    two = jnp.concatenate([chunks[2][:half] + via_one, chunks[2][half:]]).astype(BF16)
    return chunks[0] + swap(one, 1, size).astype(F32) + swap(two, 2, size).astype(F32)


def attend_kernel(query, keys_own, keys_far, value_own, value_far, order, order_own, order_far, out, totals):
    queries = query[...]
    here = order[...]

    def scores(keys, key_order):
        block = dot(keys[...].T, queries, 1, 0) * SCALE
        return jnp.where(key_order[...] <= here, block, -1e30)

    own = scores(keys_own, order_own)
    far = scores(keys_far, order_far)
    top = jnp.maximum(jnp.max(own, axis=0, keepdims=True), jnp.max(far, axis=0, keepdims=True))
    own = jnp.exp(own - top)
    far = jnp.exp(far - top)
    total = jnp.sum(own, axis=0, keepdims=True) + jnp.sum(far, axis=0, keepdims=True)
    mixed = dot(value_own[...], own.astype(BF16), 1, 0) + dot(value_far[...], far.astype(BF16), 1, 0)
    out[...] = (mixed / total).astype(BF16)
    totals[0] = top + jnp.log(total)


def attend(queries, pair_own, pair_far, order, order_far):
    width, tokens = queries.shape
    kv_heads = pair_own.shape[0] // (2 * HEAD)
    group = width // HEAD // kv_heads
    head = lambda g, e: (g * group + e, 0)
    key = lambda g, e: (g, 0)
    value = lambda g, e: (kv_heads + g, 0)
    whole = lambda g, e: (0, 0)
    kv_block = (HEAD, tokens)
    return pl.pallas_call(
        attend_kernel,
        grid=(kv_heads, group),
        in_specs=[
            pl.BlockSpec((HEAD, tokens), head),
            pl.BlockSpec(kv_block, key),
            pl.BlockSpec(kv_block, key),
            pl.BlockSpec(kv_block, value),
            pl.BlockSpec(kv_block, value),
            pl.BlockSpec((1, tokens), whole),
            pl.BlockSpec((tokens, 1), whole),
            pl.BlockSpec((tokens, 1), whole),
        ],
        out_specs=[
            pl.BlockSpec((HEAD, tokens), head),
            pl.BlockSpec((1, 1, tokens), lambda g, e: (g * group + e, 0, 0)),
        ],
        out_shape=[
            jax.ShapeDtypeStruct((width, tokens), BF16),
            jax.ShapeDtypeStruct((width // HEAD, 1, tokens), F32),
        ],
        compiler_params=pltpu.CompilerParams(vmem_limit_bytes=56 * 1024 * 1024),
        cost_estimate=pl.CostEstimate(
            flops=8 * width * tokens * tokens,
            bytes_accessed=12 * width * tokens,
            transcendentals=2 * tokens * tokens * width // HEAD,
        ),
        name="attend",
    )(queries, pair_own, pair_far, pair_own, pair_far, order[None, :], order[:, None], order_far[:, None])


def attend_back_kernel(
    query, grad, keys_own, keys_far, value_own, value_far, order, order_own, order_far, totals,
    grad_query, grad_own, grad_far, grad_value_own, grad_value_far,
):
    queries = query[...]
    grads = grad[...]
    here = order[...]
    first = pl.program_id(1) == 0

    def terms(keys, values, key_order):
        block = dot(keys[...].T, queries, 1, 0) * SCALE
        block = jnp.where(key_order[...] <= here, block, -1e30)
        probs = jnp.exp(block - totals[0])
        return probs, dot(values[...].T, grads, 1, 0)

    probs_own, back_own = terms(keys_own, value_own, order_own)
    probs_far, back_far = terms(keys_far, value_far, order_far)
    delta = jnp.sum(probs_own * back_own, axis=0, keepdims=True) + jnp.sum(
        probs_far * back_far, axis=0, keepdims=True
    )
    score_own = (probs_own * (back_own - delta)).astype(BF16)
    score_far = (probs_far * (back_far - delta)).astype(BF16)
    grad_query[...] = (
        dot(keys_own[...], score_own, 1, 0) + dot(keys_far[...], score_far, 1, 0)
    ) * SCALE
    results = (
        (grad_own, dot(queries, score_own, 1, 1) * SCALE),
        (grad_far, dot(queries, score_far, 1, 1) * SCALE),
        (grad_value_own, dot(grads, probs_own.astype(BF16), 1, 1)),
        (grad_value_far, dot(grads, probs_far.astype(BF16), 1, 1)),
    )

    @pl.when(first)
    def _():
        for ref, value in results:
            ref[...] = value

    @pl.when(jnp.logical_not(first))
    def _():
        for ref, value in results:
            ref[...] += value


def attend_back(queries, grads, pair_own, pair_far, order, order_far, totals):
    width, tokens = queries.shape
    kv_heads = pair_own.shape[0] // (2 * HEAD)
    group = width // HEAD // kv_heads
    head = lambda g, e: (g * group + e, 0)
    key = lambda g, e: (g, 0)
    value = lambda g, e: (kv_heads + g, 0)
    whole = lambda g, e: (0, 0)
    block = (HEAD, tokens)
    kv_shape = jax.ShapeDtypeStruct((kv_heads * HEAD, tokens), F32)
    return pl.pallas_call(
        attend_back_kernel,
        grid=(kv_heads, group),
        in_specs=[
            pl.BlockSpec(block, head),
            pl.BlockSpec(block, head),
            pl.BlockSpec(block, key),
            pl.BlockSpec(block, key),
            pl.BlockSpec(block, value),
            pl.BlockSpec(block, value),
            pl.BlockSpec((1, tokens), whole),
            pl.BlockSpec((tokens, 1), whole),
            pl.BlockSpec((tokens, 1), whole),
            pl.BlockSpec((1, 1, tokens), lambda g, e: (g * group + e, 0, 0)),
        ],
        out_specs=[
            pl.BlockSpec(block, head),
            pl.BlockSpec(block, key),
            pl.BlockSpec(block, key),
            pl.BlockSpec(block, key),
            pl.BlockSpec(block, key),
        ],
        out_shape=[jax.ShapeDtypeStruct((width, tokens), F32)] + [kv_shape] * 4,
        compiler_params=pltpu.CompilerParams(vmem_limit_bytes=60 * 1024 * 1024),
        cost_estimate=pl.CostEstimate(
            flops=20 * width * tokens * tokens,
            bytes_accessed=24 * width * tokens,
            transcendentals=2 * tokens * tokens * width // HEAD,
        ),
        name="attend_back",
    )(
        queries, grads, pair_own, pair_far, pair_own, pair_far,
        order[None, :], order[:, None], order_far[:, None], totals,
    )


def swiglu_terms(gate):
    sigmoid = 1.0 / (1.0 + jnp.exp(-gate))
    return sigmoid, gate * sigmoid


def feed_kernel(acts, gate_block, up_block, reduce_block, gate_out, up_out, hidden_out, out, total):
    step = pl.program_id(0)
    model = acts.shape[1]
    gate = dot(acts[...], gate_block[0].reshape(model, -1), 1, 0)
    up = dot(acts[...], up_block[0].reshape(model, -1), 1, 0)
    hidden = (swiglu_terms(gate)[1] * up).astype(BF16)
    gate_out[0] = gate
    up_out[0] = up
    hidden_out[0] = hidden
    part = dot(hidden, reduce_block[:, 0].reshape(model, -1), 1, 1)

    @pl.when(step == 0)
    def _():
        total[...] = part

    @pl.when(step > 0)
    def _():
        total[...] += part

    @pl.when(step == pl.num_programs(0) - 1)
    def _():
        out[...] = total[...].astype(BF16)


def block_specs(blocks):
    cycle, size, both, chunk = blocks.shape
    rows = both // 3 * 2
    return [
        pl.BlockSpec((1, size, rows, chunk), lambda j: (j, 0, 0, 0)),
        pl.BlockSpec((1, size, rows, chunk), lambda j: (size + j, 0, 0, 0)),
        pl.BlockSpec((cycle, 1, both - rows, chunk), lambda j: (0, j, 2, 0)),
    ]


def feed(acts, blocks):
    tokens, model = acts.shape
    cycle, size, both, chunk = blocks.shape
    unit = pl.BlockSpec((1, tokens, chunk), lambda j: (j, 0, 0))
    whole = pl.BlockSpec((tokens, model), lambda j: (0, 0))
    units = lambda kind: jax.ShapeDtypeStruct((size, tokens, chunk), kind)
    return pl.pallas_call(
        feed_kernel,
        grid=(size,),
        in_specs=[whole] + block_specs(blocks),
        out_specs=[unit, unit, unit, whole],
        out_shape=[units(F32), units(F32), units(BF16), jax.ShapeDtypeStruct((tokens, model), BF16)],
        scratch_shapes=[pltpu.VMEM((tokens, model), F32)],
        compiler_params=pltpu.CompilerParams(vmem_limit_bytes=VMEM_LIMIT),
        cost_estimate=pl.CostEstimate(
            flops=6 * tokens * model * size * chunk,
            bytes_accessed=2 * blocks.size + 4 * tokens * model + 10 * tokens * size * chunk,
            transcendentals=tokens * size * chunk,
        ),
        name="feed",
    )(acts, blocks, blocks, blocks)


def feed_back_kernel(
    grad, gate_in, up_in, gate_block, up_block, reduce_block, grad_gate_out, grad_up_out, out, total
):
    step = pl.program_id(0)
    model = grad.shape[1]
    gate = gate_in[0]
    up = up_in[0]
    grad_hidden = dot(grad[...], reduce_block[:, 0].reshape(model, -1), 1, 0)
    sigmoid, silu = swiglu_terms(gate)
    grad_gate = (grad_hidden * up * (sigmoid + silu * (1.0 - sigmoid))).astype(BF16)
    grad_up = (grad_hidden * silu).astype(BF16)
    grad_gate_out[0] = grad_gate
    grad_up_out[0] = grad_up
    part = dot(grad_gate, gate_block[0].reshape(model, -1), 1, 1)
    part += dot(grad_up, up_block[0].reshape(model, -1), 1, 1)

    @pl.when(step == 0)
    def _():
        total[...] = part

    @pl.when(step > 0)
    def _():
        total[...] += part

    @pl.when(step == pl.num_programs(0) - 1)
    def _():
        out[...] = total[...].astype(BF16)


def feed_back(grad, gate, up, blocks):
    tokens, model = grad.shape
    cycle, size, both, chunk = blocks.shape
    unit = pl.BlockSpec((1, tokens, chunk), lambda j: (j, 0, 0))
    whole = pl.BlockSpec((tokens, model), lambda j: (0, 0))
    units = jax.ShapeDtypeStruct((size, tokens, chunk), BF16)
    return pl.pallas_call(
        feed_back_kernel,
        grid=(size,),
        in_specs=[whole, unit, unit] + block_specs(blocks),
        out_specs=[unit, unit, whole],
        out_shape=[units, units, jax.ShapeDtypeStruct((tokens, model), BF16)],
        scratch_shapes=[pltpu.VMEM((tokens, model), F32)],
        compiler_params=pltpu.CompilerParams(vmem_limit_bytes=VMEM_LIMIT),
        cost_estimate=pl.CostEstimate(
            flops=6 * tokens * model * size * chunk,
            bytes_accessed=2 * blocks.size + 4 * tokens * model + 12 * tokens * size * chunk,
            transcendentals=tokens * size * chunk,
        ),
        name="feed_back",
    )(grad, gate, up, blocks, blocks, blocks)


def feed_grads_kernel(acts, grad, hidden, grad_gate, grad_up, out, acts_t, grad_t):
    step = pl.program_id(0)
    cycle, size, both, chunk = out.shape
    rows = both // 3 * 2

    @pl.when(step == 0)
    def _():
        acts_t[...] = acts[...].T
        grad_t[...] = grad[...].T

    def put(first, value):
        out[first, :, :rows, :] = value.astype(BF16).reshape(size, rows, chunk)

    put(step, dot(acts_t[...], grad_gate[0], 1, 0))
    put(size + step, dot(acts_t[...], grad_up[0], 1, 0))
    last = dot(grad_t[...], hidden[0], 1, 0)
    out[:, step, rows:, :] = last.astype(BF16).reshape(cycle, both - rows, chunk)


def feed_grads(acts, grad, hidden, grad_gate, grad_up, shape):
    tokens, model = acts.shape
    cycle, size, both, chunk = shape
    unit = pl.BlockSpec((1, tokens, chunk), lambda j: (j, 0, 0))
    whole = pl.BlockSpec((tokens, model), lambda j: (0, 0))
    return pl.pallas_call(
        feed_grads_kernel,
        grid=(size,),
        in_specs=[whole, whole, unit, unit, unit],
        out_specs=pl.BlockSpec(shape, lambda j: (0, 0, 0, 0)),
        out_shape=jax.ShapeDtypeStruct(shape, BF16),
        scratch_shapes=[pltpu.VMEM((model, tokens), BF16)] * 2,
        compiler_params=pltpu.CompilerParams(vmem_limit_bytes=VMEM_LIMIT),
        cost_estimate=pl.CostEstimate(
            flops=6 * tokens * model * size * chunk,
            bytes_accessed=2 * cycle * size * both * chunk + 4 * tokens * model + 6 * tokens * size * chunk,
            transcendentals=0,
        ),
        name="feed_grads",
    )(acts, grad, hidden, grad_gate, grad_up)


def rotate(tensor, cosine, sine):
    half = HEAD // 2
    tokens = tensor.shape[1]
    split = tensor.reshape(-1, 2, half, tokens)
    first, second = (split[:, 0], split[:, 1])
    return jnp.stack(
        [first * cosine - second * sine, second * cosine + first * sine], axis=1
    ).reshape(-1, tokens)


def inverse_rms(stream):
    return lax.rsqrt(jnp.mean(stream * stream, axis=-1, keepdims=True) + EPS)


def norm_back(stream, gain, grad):
    scale = inverse_rms(stream)
    inner = jnp.mean(stream * gain * grad, axis=-1, keepdims=True)
    grad_stream = scale * (gain * grad) - stream * (scale * scale * scale * inner)
    return grad_stream, jnp.sum(grad * stream * scale, axis=0)


def adamw(weight, moment, variance, grad, rate, decay):
    moment = DECAY_FIRST * moment + (1.0 - DECAY_FIRST) * grad
    variance = DECAY_SECOND * variance + (1.0 - DECAY_SECOND) * grad * grad
    update = (
        moment
        / (1.0 - DECAY_FIRST**STEP)
        / (jnp.sqrt(variance / (1.0 - DECAY_SECOND**STEP)) + ADAM_EPS)
    )
    return (weight - rate * (update + decay * weight), moment, variance)


def adamw_kernel(weight, moment, variance, grad, *refs):
    new = adamw(
        weight[0], moment[0], variance[0], grad[...].astype(F32), RATE_MATRIX, WEIGHT_DECAY
    )
    for ref, value in zip(refs[-3:], new):
        ref[0] = value


def adamw_layer(state, grad, layer, earlier):
    rows, cols = grad.shape
    steps = 4 if rows % 64 == 0 else 1
    block = pl.BlockSpec((1, rows // steps, cols), lambda j: (layer, j, 0))
    held = pl.BlockSpec(memory_space=pl.ANY)
    shape = jax.ShapeDtypeStruct(state[0].shape, F32)
    return pl.pallas_call(
        adamw_kernel,
        grid=(steps,),
        in_specs=[block] * 3
        + [pl.BlockSpec((rows // steps, cols), lambda j: (j, 0))]
        + [held] * len(earlier),
        out_specs=[block] * 3,
        out_shape=[shape] * 3,
        input_output_aliases={4 + k: k for k in range(len(earlier))},
        compiler_params=pltpu.CompilerParams(vmem_limit_bytes=VMEM_LIMIT),
        cost_estimate=pl.CostEstimate(
            flops=20 * rows * cols, bytes_accessed=26 * rows * cols, transcendentals=2 * rows * cols
        ),
        name="adamw",
    )(*state, grad, *earlier)


def turned(arrays):
    return tuple(jnp.swapaxes(array, 1, 2) for array in arrays)


def body(
    block_in,
    cotangent,
    positions,
    attend_weight,
    attend_moment,
    attend_variance,
    output_weight,
    output_moment,
    output_variance,
    expand_weight,
    expand_moment,
    expand_variance,
    reduce_weight,
    reduce_moment,
    reduce_variance,
    gains,
    gains_moment,
    gains_variance,
):
    size = lax.axis_size("fsdp")
    cycle = lax.axis_size("ctx")
    row = lax.axis_index("fsdp")
    column = lax.axis_index("ctx")
    model = block_in.shape[2]
    att_rows, att_cols = attend_weight.shape[1:]
    out_rows, out_cols = output_weight.shape[1:]
    exp_rows, exp_cols = expand_weight.shape[1:]
    red_rows, red_cols = reduce_weight.shape[1:]
    chunk = exp_cols // size
    gain_cols = gains.shape[1]
    plane = column // 2
    by_half = attend_pairs(size, cycle)
    holds_values = column >= size + size // 2
    mixed_up = jnp.logical_and(column >= size, row % 2 == 1)
    half = att_cols // 2
    others = jnp.bitwise_xor(row, jnp.arange(size))

    def send_attend():
        low = attend_weight.astype(BF16)
        lead, tail = exchange_attend(
            low[..., :half], low[..., half:], holds_values, mixed_up, by_half[0], by_half[1]
        )
        return jnp.concatenate([lead, tail], axis=2)

    def exchange_rows(parts):
        parts = exchange(jnp.take(parts, others, axis=0), "fsdp", 1, size)
        return jnp.take(parts, others, axis=0)

    def send_feed(layer, *events):
        expand, reduce = after((expand_weight[layer], reduce_weight[layer]), *events)
        expand = jnp.transpose(expand.astype(BF16).reshape(exp_rows, size, chunk), (1, 0, 2))
        reduce = jnp.transpose(reduce.astype(BF16).reshape(size, chunk, red_cols), (0, 2, 1))
        return exchange_rows(jnp.concatenate([expand, reduce], axis=1))

    def gather(payload):
        return lax.all_gather(payload, "ctx", axis=0, tiled=False)

    pieces = []
    rest = gains
    for _ in range(GAIN_PARTS):
        part = rest.astype(BF16)
        rest = rest - part.astype(F32)
        pieces.append(part)
    gain_own = jnp.stack(pieces)
    gain_all = jnp.stack([gain_own] + [swap(gain_own, k, size) for k in range(1, size)])
    gain_all = jnp.take(gain_all, others, axis=0)
    gain_flat = gain_all.reshape(-1, att_cols)
    gain_used = gain_flat.shape[0]

    attend_sent = send_attend()
    tokens = block_in.shape[1]
    digits = jnp.stack([positions[0] // RUN, positions[0] % RUN], axis=1).astype(BF16)
    digits = jnp.pad(digits, ((0, 0), (0, LANES - digits.shape[1])))
    stream_low = to_plane(jnp.concatenate([block_in[0], digits], axis=1), size, row, plane)
    payload = jnp.concatenate(
        [attend_sent, jnp.swapaxes(output_weight.astype(BF16), 1, 2)], axis=1
    ).reshape(-1, att_cols)
    gain_rows = jnp.pad(gain_flat, ((0, GAIN_ROWS - gain_used), (0, 0)))
    payload = after(jnp.concatenate([payload, gain_rows]), stream_low)
    attn_parts = gather(payload)
    mlp_parts = [None] * LAYERS
    payload = send_feed(0, payload)
    mlp_parts[0] = gather(payload)
    stream_all = gather_tokens(after(stream_low, payload), size)
    order = stream_all[:, model : model + 2].astype(jnp.int32)
    order = order[:, 0] * RUN + order[:, 1]
    order_far = swap_core(order, cycle)
    stream_first = stream_all[:, :model]
    stream_low = stream_low[:, :model]
    payload = send_feed(1, payload, stream_all)
    mlp_parts[1] = gather(payload)
    back_low = to_plane(after(cotangent[0], payload), size, row, plane)
    back_all = gather_tokens(back_low, size)

    attn_rows = att_rows + out_cols
    gain_table = attn_parts[:, LAYERS * attn_rows : LAYERS * attn_rows + gain_used]
    gain_table = gain_table.reshape(cycle, size, GAIN_PARTS, 2 * LAYERS, gain_cols).astype(F32)
    gain_table = gain_table[:, :, 0] + gain_table[:, :, 1] + gain_table[:, :, 2]
    gain_table = jnp.transpose(gain_table, (2, 1, 0, 3)).reshape(2 * LAYERS, model)

    def attn_weights(layer):
        part = attn_parts[:, layer * attn_rows : (layer + 1) * attn_rows]
        block = part[:, :att_rows]
        return (
            block[:size].reshape(model, att_cols),
            block[size:].reshape(model, att_cols),
            part[:, att_rows : att_rows + out_cols].reshape(model, out_rows),
        )

    freq = THETA ** (-2.0 * jnp.arange(HEAD // 2, dtype=F32) / HEAD)
    angle = freq[:, None] * order.astype(F32)[None, :]
    cosine, sine = (jnp.cos(angle), jnp.sin(angle))

    stream = stream_low.astype(F32)
    stream_first = stream_first.astype(F32)
    saved = []
    for layer in range(LAYERS):
        gain_attend, gain_mix = (gain_table[2 * layer], gain_table[2 * layer + 1])
        query_weight, pair_weight, output_t = attn_weights(layer)
        if layer == 0:
            acts = (stream_first * inverse_rms(stream_first) * gain_attend).astype(BF16)
        else:
            acts = gather_tokens((stream * inverse_rms(stream) * gain_attend).astype(BF16), size)
        queries = rotate(dot(query_weight, acts, 0, 1), cosine, sine).astype(BF16)
        pair = dot(pair_weight, acts, 0, 1)
        pair = jnp.concatenate(
            [rotate(pair[: pair.shape[0] // 2], cosine, sine), pair[pair.shape[0] // 2 :]]
        ).astype(BF16)
        pair_far = swap_core(pair, cycle)
        mixed, totals = attend(queries, pair, pair_far, order, order_far)
        middle = stream + scatter_tokens(dot(mixed, output_t, 0, 1), size)
        middle_low = gather_tokens((middle * inverse_rms(middle) * gain_mix).astype(BF16), size)
        if layer == 0:
            mlp_parts[0] = after(mlp_parts[0], back_all)
        gate, up, hidden, partial = feed(middle_low, mlp_parts[layer])
        if layer < LAYERS - 1:
            stream_next = middle + scatter_tokens(partial, size)
        saved.append((stream, acts, queries, pair, pair_far, mixed, totals, middle, middle_low, gate, up, hidden))
        stream = stream_next

    back = back_low.astype(F32)
    gain_grads = [None] * (2 * LAYERS)

    def reduce(payload):
        return lax.psum_scatter(payload, "ctx", scatter_dimension=0, tiled=False)

    mlp_grads = {}
    attn_grads = {}

    for layer in reversed(range(LAYERS)):
        stream, acts, queries, pair, pair_far, mixed, totals, middle, middle_low, gate, up, hidden = saved[layer]
        gain_attend, gain_mix = (gain_table[2 * layer], gain_table[2 * layer + 1])
        query_weight, pair_weight, output_t = attn_weights(layer)
        if layer < LAYERS - 1:
            back_all = gather_tokens(back.astype(BF16), size)
            back_all, mlp_grads[layer + 1] = lax.optimization_barrier((back_all, mlp_grads[layer + 1]))
            attn_grads[layer + 1] = reduce(after(attn_payload, mlp_grads[layer + 1]))
        grad_gate, grad_up, grad_partial = feed_back(back_all, gate, up, mlp_parts[layer])
        payload = feed_grads(
            middle_low, back_all, hidden, grad_gate, grad_up, mlp_parts[layer].shape
        )
        grad_middle = scatter_tokens(grad_partial, size)
        payload, grad_middle = lax.optimization_barrier((payload, grad_middle))
        if layer == LAYERS - 1:
            mlp_grads[layer] = reduce(payload)
            last_middle, last_partial = (middle, partial)
        change, gain_grads[2 * layer + 1] = norm_back(middle, gain_mix, grad_middle)
        back = back + change
        back_attend = gather_tokens(back.astype(BF16), size)
        if layer < LAYERS - 1:
            back_attend, attn_grads[layer + 1] = lax.optimization_barrier(
                (back_attend, attn_grads[layer + 1])
            )
            mlp_grads[layer] = reduce(after(payload, attn_grads[layer + 1]))
        grad_mixed = dot(output_t, back_attend, 0, 1).astype(BF16)
        grad_query, key_own, key_far, value_own, value_far = attend_back(
            queries, grad_mixed, pair, pair_far, order, order_far, totals
        )
        from_far = swap_core(jnp.concatenate([key_far, value_far]).astype(BF16), cycle).astype(F32)
        rows_kv = key_own.shape[0]
        grad_key = key_own + from_far[:rows_kv]
        grad_value = value_own + from_far[rows_kv:]
        grad_query = rotate(grad_query.astype(BF16).astype(F32), cosine, -sine).astype(BF16)
        grad_key = rotate(grad_key.astype(BF16).astype(F32), cosine, -sine).astype(BF16)
        grad_pair = jnp.concatenate([grad_key, grad_value.astype(BF16)])
        grad_acts = dot(grad_query, query_weight, 0, 1) + dot(grad_pair, pair_weight, 0, 1)
        parts = [
            jnp.concatenate([dot(acts, grad_query, 0, 1), dot(acts, grad_pair, 0, 1)])
            .astype(BF16)
            .reshape(cycle, att_rows, att_cols),
            dot(back_attend, mixed, 0, 1).astype(BF16).reshape(cycle, out_cols, out_rows),
        ]
        grad_stream = scatter_tokens(grad_acts, size)
        change, gain_grads[2 * layer] = norm_back(stream, gain_attend, grad_stream)
        back = back + change
        if layer == 0:
            gain_grads[0] = jnp.sum(grad_acts * stream_first * inverse_rms(stream_first), axis=0)
            table = jnp.stack(gain_grads).reshape(2 * LAYERS, size, cycle, gain_cols)
            table = jnp.transpose(table, (2, 1, 0, 3)).astype(BF16).reshape(cycle, -1, att_cols)
            fill = jnp.zeros((cycle, GAIN_ROWS - table.shape[1], att_cols), BF16)
            parts += [table, fill]
        attn_payload, back = lax.optimization_barrier((jnp.concatenate(parts, axis=1), back))
    states = {
        "attend": (attend_weight, attend_moment, attend_variance),
        "output": turned((output_weight, output_moment, output_variance)),
        "expand": (expand_weight, expand_moment, expand_variance),
        "reduce": turned((reduce_weight, reduce_moment, reduce_variance)),
    }
    renewed = {name: () for name in states}

    def renew(name, layer, grad):
        renewed[name] = adamw_layer(states[name], grad, layer, renewed[name])

    def renew_feed(layer, mlp_grad):
        mlp_grad = exchange_rows(mlp_grad)
        expand = jnp.transpose(mlp_grad[:, :exp_rows], (1, 0, 2)).reshape(exp_rows, exp_cols)
        reduce = jnp.transpose(mlp_grad[:, exp_rows:], (1, 0, 2)).reshape(red_cols, red_rows)
        renew("expand", layer, expand)
        renew("reduce", layer, reduce)

    def renew_attend(layer, attn_grad):
        block = attn_grad[:att_rows]
        lead, tail = exchange_attend(
            block[:, :half],
            block[:, half:],
            mixed_up,
            holds_values,
            backwards(by_half[0]),
            backwards(by_half[1]),
        )
        renew("attend", layer, jnp.concatenate([lead, tail], axis=1))
        renew("output", layer, attn_grad[att_rows : att_rows + out_cols])

    for layer in reversed(range(1, LAYERS)):
        renew_feed(layer, after(mlp_grads[layer], attn_payload))
    block_out = last_middle + scatter_tokens(after(last_partial, attn_payload), size)
    attn_payload, renewed, block_out, mlp_grads[0] = lax.optimization_barrier(
        (attn_payload, renewed, block_out, mlp_grads[0])
    )
    attn_grads[0] = reduce(attn_payload)
    for layer in reversed(range(1, LAYERS)):
        renew_attend(layer, after(attn_grads[layer], attn_payload))
    renew_feed(0, mlp_grads[0])
    outs = jnp.concatenate([block_out, back], axis=1).astype(BF16)
    outs = from_plane(after(outs, attn_payload), size, row, plane)
    attn_grads[0], renewed, outs = lax.optimization_barrier((attn_grads[0], renewed, outs))
    renew_attend(0, attn_grads[0])
    grad_gains = attn_grads[0][att_rows + out_cols : att_rows + out_cols + table.shape[1]]
    grad_gains = grad_gains.astype(F32).reshape(size, 2 * LAYERS, gain_cols)
    grad_gains = jnp.take(grad_gains, others, axis=0)
    total = grad_gains[0]
    for k in range(1, size):
        total = total + swap(grad_gains[k], k, size)
    grad_gains = total

    for name in ("output", "reduce"):
        renewed[name] = turned(renewed[name])
    results = [value for name in states for value in renewed[name]]
    results += list(adamw(gains, gains_moment, gains_variance, grad_gains, RATE_GAIN, 0.0))
    outs = outs.astype(F32)
    return (outs[None, :, :model], outs[None, :, model:], *results)


def solution(mesh):
    tokens = P("fsdp", "ctx", None)
    matrix = P(None, "fsdp", "ctx")
    gain = P(None, ("fsdp", "ctx"))
    return jax.shard_map(
        body,
        mesh=mesh,
        in_specs=(tokens, tokens, P("fsdp", "ctx")) + (matrix,) * 12 + (gain,) * 3,
        out_specs=(tokens, tokens) + (matrix,) * 12 + (gain,) * 3,
        check_vma=False,
    )
```

```python
import functools
import math

import jax
import jax.numpy as jnp
from jax import lax
from jax.experimental import pallas as pl
from jax.experimental.pallas import tpu as pltpu
from jax.sharding import PartitionSpec as P

HEADS = 16
KV_HEADS = 8
HEAD = 96
LAYERS = 2
STEP = 10

EPS = 1e-05
THETA = 100000.0
DECAY_FIRST = 0.9
DECAY_SECOND = 0.95
ADAM_EPS = 1e-08
WEIGHT_DECAY = 0.1
RATE_MATRIX = 0.06
RATE_GAIN = 0.6

BF16 = jnp.bfloat16
F32 = jnp.float32
SCALE = 1.0 / math.sqrt(HEAD)
GAIN_PARTS = 3
GAIN_ROWS = 16
RUN = 64
LANES = 128
BOTH = ("fsdp", "ctx")
VMEM_LIMIT = 60 * 1024 * 1024


def dot(left, right, contract_left, contract_right):
    return lax.dot_general(
        left,
        right,
        (((contract_left,), (contract_right,)), ((), ())),
        preferred_element_type=F32,
    )


def after(value, *events):
    return lax.optimization_barrier((value, *events))[0]


def swap(value, distance, size):
    return lax.ppermute(value, "fsdp", [(i, i ^ distance) for i in range(size)])


def swap_core(value, cycle):
    return lax.ppermute(value, "ctx", [(i, i ^ 1) for i in range(cycle)])


def exchange(parts, axis, step, size):
    cycle = lax.axis_size(axis)
    received = [parts[0]]
    for k in range(1, size):
        received.append(lax.ppermute(parts[k], axis, [(i, i ^ (k * step)) for i in range(cycle)]))
    return received


def parts_for(value, me, size):
    return [
        lax.dynamic_index_in_dim(value, jnp.bitwise_xor(me, k), 0, keepdims=False)
        for k in range(size)
    ]


def parts_from(parts, me):
    value = jnp.zeros((len(parts), *parts[0].shape), parts[0].dtype)
    for k, part in enumerate(parts):
        value = lax.dynamic_update_index_in_dim(value, part, jnp.bitwise_xor(me, k), 0)
    return value


def to_plane_rows(parts, size, row):
    return parts_from(exchange(parts, "fsdp", 1, size), row)


def to_plane(parts, size, plane):
    parts = exchange(parts_for(parts, plane, size), "ctx", 2, size)
    return jnp.concatenate(parts)


def from_plane(value, size, row, plane):
    parts = exchange(value.reshape(size, -1, value.shape[-1]), "ctx", 2, size)
    parts = exchange(parts_for(parts_from(parts, plane), row, size), "fsdp", 1, size)
    return parts_from(parts, row).reshape(value.shape)


def attend_pairs(size, cycle):
    both = []
    for odd in range(2):
        pairs = []
        for row in range(size):
            for f in range(size):
                pairs.append((row * cycle + f, f * cycle + row))
            for k in range(size // 2):
                key_to, value_to = (2 * k + odd, 2 * k + 1 - odd)
                pairs.append((row * cycle + size + k, key_to * cycle + size + row))
                pairs.append((row * cycle + size + size // 2 + k, value_to * cycle + size + row))
        both.append(pairs)
    return both


def backwards(pairs):
    return [(target, source) for source, target in pairs]


def exchange_attend(first, second, flip_here, flip_there, pairs_first, pairs_second):
    lead = jnp.where(flip_here, second, first)
    tail = jnp.where(flip_here, first, second)
    lead = lax.ppermute(lead, BOTH, pairs_first)
    tail = lax.ppermute(tail, BOTH, pairs_second)
    return jnp.where(flip_there, tail, lead), jnp.where(flip_there, lead, tail)


def gather_tokens(piece, size):
    if size != 4:
        return jnp.concatenate([piece] + [swap(piece, k, size) for k in range(1, size)])
    half = piece.shape[0] // 2
    one = swap(piece, 1, size)
    two = swap(piece, 2, size)
    three_top = swap(one[:half], 2, size)
    three_low = swap(two[half:], 1, size)
    return jnp.concatenate([piece, one, two, three_top, three_low])


def scatter_tokens(partial, size):
    tokens = partial.shape[0] // size
    chunks = [partial[k * tokens : (k + 1) * tokens].astype(F32) for k in range(size)]
    if size != 4:
        total = chunks[0]
        for k in range(1, size):
            total = total + swap(chunks[k].astype(BF16), k, size).astype(F32)
        return total
    half = tokens // 2
    far = chunks[3].astype(BF16)
    via_one = swap(far[:half], 1, size).astype(F32)
    via_two = swap(far[half:], 2, size).astype(F32)
    one = jnp.concatenate([chunks[1][:half], chunks[1][half:] + via_two]).astype(BF16)
    two = jnp.concatenate([chunks[2][:half] + via_one, chunks[2][half:]]).astype(BF16)
    return chunks[0] + swap(one, 1, size).astype(F32) + swap(two, 2, size).astype(F32)


def attend_kernel(query, keys_own, keys_far, value_own, value_far, order, order_own, order_far, out, totals):
    queries = query[...]
    here = order[...]

    def scores(keys, key_order):
        block = dot(keys[...].T, queries, 1, 0) * SCALE
        return jnp.where(key_order[...] <= here, block, -1e30)

    own = scores(keys_own, order_own)
    far = scores(keys_far, order_far)
    top = jnp.maximum(jnp.max(own, axis=0, keepdims=True), jnp.max(far, axis=0, keepdims=True))
    own = jnp.exp(own - top)
    far = jnp.exp(far - top)
    total = jnp.sum(own, axis=0, keepdims=True) + jnp.sum(far, axis=0, keepdims=True)
    mixed = dot(value_own[...], own.astype(BF16), 1, 0) + dot(value_far[...], far.astype(BF16), 1, 0)
    out[...] = (mixed / total).astype(BF16)
    totals[0] = top + jnp.log(total)


def attend(queries, pair_own, pair_far, order, order_far):
    width, tokens = queries.shape
    kv_heads = pair_own.shape[0] // (2 * HEAD)
    group = width // HEAD // kv_heads
    head = lambda g, e: (g * group + e, 0)
    key = lambda g, e: (g, 0)
    value = lambda g, e: (kv_heads + g, 0)
    whole = lambda g, e: (0, 0)
    kv_block = (HEAD, tokens)
    return pl.pallas_call(
        attend_kernel,
        grid=(kv_heads, group),
        in_specs=[
            pl.BlockSpec((HEAD, tokens), head),
            pl.BlockSpec(kv_block, key),
            pl.BlockSpec(kv_block, key),
            pl.BlockSpec(kv_block, value),
            pl.BlockSpec(kv_block, value),
            pl.BlockSpec((1, tokens), whole),
            pl.BlockSpec((tokens, 1), whole),
            pl.BlockSpec((tokens, 1), whole),
        ],
        out_specs=[
            pl.BlockSpec((HEAD, tokens), head),
            pl.BlockSpec((1, 1, tokens), lambda g, e: (g * group + e, 0, 0)),
        ],
        out_shape=[
            jax.ShapeDtypeStruct((width, tokens), BF16),
            jax.ShapeDtypeStruct((width // HEAD, 1, tokens), F32),
        ],
        compiler_params=pltpu.CompilerParams(vmem_limit_bytes=56 * 1024 * 1024),
        cost_estimate=pl.CostEstimate(
            flops=8 * width * tokens * tokens,
            bytes_accessed=12 * width * tokens,
            transcendentals=2 * tokens * tokens * width // HEAD,
        ),
        name="attend",
    )(queries, pair_own, pair_far, pair_own, pair_far, order[None, :], order[:, None], order_far[:, None])


def attend_back_kernel(
    query, grad, keys_own, keys_far, value_own, value_far, order, order_own, order_far, totals,
    grad_query, grad_own, grad_far, grad_value_own, grad_value_far,
):
    queries = query[...]
    grads = grad[...]
    here = order[...]
    first = pl.program_id(1) == 0

    def terms(keys, values, key_order):
        block = dot(keys[...].T, queries, 1, 0) * SCALE
        block = jnp.where(key_order[...] <= here, block, -1e30)
        probs = jnp.exp(block - totals[0])
        return probs, dot(values[...].T, grads, 1, 0)

    probs_own, back_own = terms(keys_own, value_own, order_own)
    probs_far, back_far = terms(keys_far, value_far, order_far)
    delta = jnp.sum(probs_own * back_own, axis=0, keepdims=True) + jnp.sum(
        probs_far * back_far, axis=0, keepdims=True
    )
    score_own = (probs_own * (back_own - delta)).astype(BF16)
    score_far = (probs_far * (back_far - delta)).astype(BF16)
    grad_query[...] = (
        dot(keys_own[...], score_own, 1, 0) + dot(keys_far[...], score_far, 1, 0)
    ) * SCALE
    results = (
        (grad_own, dot(queries, score_own, 1, 1) * SCALE),
        (grad_far, dot(queries, score_far, 1, 1) * SCALE),
        (grad_value_own, dot(grads, probs_own.astype(BF16), 1, 1)),
        (grad_value_far, dot(grads, probs_far.astype(BF16), 1, 1)),
    )

    @pl.when(first)
    def _():
        for ref, value in results:
            ref[...] = value

    @pl.when(jnp.logical_not(first))
    def _():
        for ref, value in results:
            ref[...] += value


def attend_back(queries, grads, pair_own, pair_far, order, order_far, totals):
    width, tokens = queries.shape
    kv_heads = pair_own.shape[0] // (2 * HEAD)
    group = width // HEAD // kv_heads
    head = lambda g, e: (g * group + e, 0)
    key = lambda g, e: (g, 0)
    value = lambda g, e: (kv_heads + g, 0)
    whole = lambda g, e: (0, 0)
    block = (HEAD, tokens)
    kv_shape = jax.ShapeDtypeStruct((kv_heads * HEAD, tokens), F32)
    return pl.pallas_call(
        attend_back_kernel,
        grid=(kv_heads, group),
        in_specs=[
            pl.BlockSpec(block, head),
            pl.BlockSpec(block, head),
            pl.BlockSpec(block, key),
            pl.BlockSpec(block, key),
            pl.BlockSpec(block, value),
            pl.BlockSpec(block, value),
            pl.BlockSpec((1, tokens), whole),
            pl.BlockSpec((tokens, 1), whole),
            pl.BlockSpec((tokens, 1), whole),
            pl.BlockSpec((1, 1, tokens), lambda g, e: (g * group + e, 0, 0)),
        ],
        out_specs=[
            pl.BlockSpec(block, head),
            pl.BlockSpec(block, key),
            pl.BlockSpec(block, key),
            pl.BlockSpec(block, key),
            pl.BlockSpec(block, key),
        ],
        out_shape=[jax.ShapeDtypeStruct((width, tokens), F32)] + [kv_shape] * 4,
        compiler_params=pltpu.CompilerParams(vmem_limit_bytes=60 * 1024 * 1024),
        cost_estimate=pl.CostEstimate(
            flops=20 * width * tokens * tokens,
            bytes_accessed=24 * width * tokens,
            transcendentals=2 * tokens * tokens * width // HEAD,
        ),
        name="attend_back",
    )(
        queries, grads, pair_own, pair_far, pair_own, pair_far,
        order[None, :], order[:, None], order_far[:, None], totals,
    )


def swiglu_terms(gate):
    sigmoid = 1.0 / (1.0 + jnp.exp(-gate))
    return sigmoid, gate * sigmoid


def feed_kernel(acts, gate_block, up_block, reduce_block, gate_out, up_out, hidden_out, out, total):
    step = pl.program_id(0)
    model = acts.shape[1]
    gate = dot(acts[...], gate_block[0].reshape(model, -1), 1, 0)
    up = dot(acts[...], up_block[0].reshape(model, -1), 1, 0)
    hidden = (swiglu_terms(gate)[1] * up).astype(BF16)
    gate_out[0] = gate.astype(BF16)
    up_out[0] = up.astype(BF16)
    hidden_out[0] = hidden
    part = dot(hidden, reduce_block[:, 0].reshape(model, -1), 1, 1)

    @pl.when(step == 0)
    def _():
        total[...] = part

    @pl.when(step > 0)
    def _():
        total[...] += part

    @pl.when(step == pl.num_programs(0) - 1)
    def _():
        out[...] = total[...].astype(BF16)


def block_specs(blocks):
    cycle, size, both, chunk = blocks.shape
    rows = both // 3 * 2
    return [
        pl.BlockSpec((1, size, rows, chunk), lambda j: (j, 0, 0, 0)),
        pl.BlockSpec((1, size, rows, chunk), lambda j: (size + j, 0, 0, 0)),
        pl.BlockSpec((cycle, 1, both - rows, chunk), lambda j: (0, j, 2, 0)),
    ]


def feed(acts, blocks):
    tokens, model = acts.shape
    cycle, size, both, chunk = blocks.shape
    unit = pl.BlockSpec((1, tokens, chunk), lambda j: (j, 0, 0))
    whole = pl.BlockSpec((tokens, model), lambda j: (0, 0))
    units = jax.ShapeDtypeStruct((size, tokens, chunk), BF16)
    return pl.pallas_call(
        feed_kernel,
        grid=(size,),
        in_specs=[whole] + block_specs(blocks),
        out_specs=[unit, unit, unit, whole],
        out_shape=[units, units, units, jax.ShapeDtypeStruct((tokens, model), BF16)],
        scratch_shapes=[pltpu.VMEM((tokens, model), F32)],
        compiler_params=pltpu.CompilerParams(vmem_limit_bytes=VMEM_LIMIT),
        cost_estimate=pl.CostEstimate(
            flops=6 * tokens * model * size * chunk,
            bytes_accessed=2 * blocks.size + 4 * tokens * model + 6 * tokens * size * chunk,
            transcendentals=tokens * size * chunk,
        ),
        name="feed",
    )(acts, blocks, blocks, blocks)


def put_grads(out, units_buf, model_buf, sems, acts, grad, hidden, grad_gate, grad_up):
    step = pl.program_id(0)
    last = pl.num_programs(0) - 1
    slot = lax.rem(step, 2)
    cycle, size, both, chunk = out.shape
    rows = both // 3 * 2

    def copies(j, at):
        return (
            pltpu.make_async_copy(units_buf.at[at, 0], out.at[j, :, pl.ds(0, rows), :], sems.at[at, 0]),
            pltpu.make_async_copy(units_buf.at[at, 1], out.at[size + j, :, pl.ds(0, rows), :], sems.at[at, 1]),
            pltpu.make_async_copy(model_buf.at[at], out.at[:, j, pl.ds(rows, both - rows), :], sems.at[at, 2]),
        )

    @pl.when(step >= 2)
    def _():
        for copy in copies(step - 2, slot):
            copy.wait()

    units_buf[slot, 0] = dot(acts[...], grad_gate, 0, 0).astype(BF16).reshape(size, rows, chunk)
    units_buf[slot, 1] = dot(acts[...], grad_up, 0, 0).astype(BF16).reshape(size, rows, chunk)
    model_buf[slot] = dot(grad[...], hidden, 0, 0).astype(BF16).reshape(cycle, both - rows, chunk)
    for copy in copies(step, slot):
        copy.start()

    @pl.when(step == last)
    def _():
        for copy in copies(step - 1, 1 - slot):
            copy.wait()
        for copy in copies(step, slot):
            copy.wait()


def grads_scratch(shape):
    cycle, size, both, chunk = shape
    rows = both // 3 * 2
    return [
        pltpu.VMEM((2, 2, size, rows, chunk), BF16),
        pltpu.VMEM((2, cycle, both - rows, chunk), BF16),
        pltpu.SemaphoreType.DMA((2, 3)),
    ]


def feed_last_kernel(
    acts, grad, gate_block, up_block, reduce_block,
    hidden_out, grad_gate_out, grad_up_out, out, units_buf, model_buf, sems,
):
    model = acts.shape[1]
    gate = dot(acts[...], gate_block[0].reshape(model, -1), 1, 0)
    up = dot(acts[...], up_block[0].reshape(model, -1), 1, 0)
    grad_hidden = dot(grad[...], reduce_block[:, 0].reshape(model, -1), 1, 0)
    sigmoid, silu = swiglu_terms(gate)
    hidden = (silu * up).astype(BF16)
    grad_gate = (grad_hidden * up * (sigmoid + silu * (1.0 - sigmoid))).astype(BF16)
    grad_up = (grad_hidden * silu).astype(BF16)
    hidden_out[0] = hidden
    grad_gate_out[0] = grad_gate
    grad_up_out[0] = grad_up
    put_grads(out, units_buf, model_buf, sems, acts, grad, hidden, grad_gate, grad_up)


def feed_last(acts, grad, blocks):
    tokens, model = acts.shape
    cycle, size, both, chunk = blocks.shape
    unit = pl.BlockSpec((1, tokens, chunk), lambda j: (j, 0, 0))
    whole = pl.BlockSpec((tokens, model), lambda j: (0, 0))
    units = jax.ShapeDtypeStruct((size, tokens, chunk), BF16)
    return pl.pallas_call(
        feed_last_kernel,
        grid=(size,),
        in_specs=[whole, whole] + block_specs(blocks),
        out_specs=[unit, unit, unit, pl.BlockSpec(memory_space=pl.ANY)],
        out_shape=[units, units, units, jax.ShapeDtypeStruct(blocks.shape, BF16)],
        scratch_shapes=grads_scratch(blocks.shape),
        compiler_params=pltpu.CompilerParams(vmem_limit_bytes=VMEM_LIMIT),
        cost_estimate=pl.CostEstimate(
            flops=12 * tokens * model * size * chunk,
            bytes_accessed=4 * blocks.size + 4 * tokens * model + 6 * tokens * size * chunk,
            transcendentals=tokens * size * chunk,
        ),
        name="feed_last",
    )(acts, grad, blocks, blocks, blocks)


def feed_turn_kernel(
    acts, grad, hidden, gate_in, up_in, reduce_block,
    grad_gate_out, grad_up_out, out, units_buf, model_buf, sems,
):
    model = acts.shape[1]
    gate = gate_in[0].astype(F32)
    up = up_in[0].astype(F32)
    grad_hidden = dot(grad[...], reduce_block[:, 0].reshape(model, -1), 1, 0)
    sigmoid, silu = swiglu_terms(gate)
    grad_gate = (grad_hidden * up * (sigmoid + silu * (1.0 - sigmoid))).astype(BF16)
    grad_up = (grad_hidden * silu).astype(BF16)
    grad_gate_out[0] = grad_gate
    grad_up_out[0] = grad_up
    put_grads(out, units_buf, model_buf, sems, acts, grad, hidden[0], grad_gate, grad_up)


def feed_turn(acts, grad, hidden, gate, up, blocks):
    tokens, model = acts.shape
    cycle, size, both, chunk = blocks.shape
    unit = pl.BlockSpec((1, tokens, chunk), lambda j: (j, 0, 0))
    whole = pl.BlockSpec((tokens, model), lambda j: (0, 0))
    units = jax.ShapeDtypeStruct((size, tokens, chunk), BF16)
    return pl.pallas_call(
        feed_turn_kernel,
        grid=(size,),
        in_specs=[whole, whole, unit, unit, unit] + block_specs(blocks)[2:],
        out_specs=[unit, unit, pl.BlockSpec(memory_space=pl.ANY)],
        out_shape=[units, units, jax.ShapeDtypeStruct(blocks.shape, BF16)],
        scratch_shapes=grads_scratch(blocks.shape),
        compiler_params=pltpu.CompilerParams(vmem_limit_bytes=VMEM_LIMIT),
        cost_estimate=pl.CostEstimate(
            flops=8 * tokens * model * size * chunk,
            bytes_accessed=3 * blocks.size + 4 * tokens * model + 10 * tokens * size * chunk,
            transcendentals=tokens * size * chunk,
        ),
        name="feed_turn",
    )(acts, grad, hidden, gate, up, blocks)


def sum_steps(total, out, part):
    step = pl.program_id(0)

    @pl.when(step == 0)
    def _():
        total[...] = part

    @pl.when(step > 0)
    def _():
        total[...] += part

    @pl.when(step == pl.num_programs(0) - 1)
    def _():
        out[...] = total[...].astype(BF16)


def feed_input_kernel(grad_gate, grad_up, gate_block, up_block, out, total):
    model = out.shape[1]
    part = dot(grad_gate[0], gate_block[0].reshape(model, -1), 1, 1)
    part += dot(grad_up[0], up_block[0].reshape(model, -1), 1, 1)
    sum_steps(total, out, part)


def feed_out_kernel(hidden, reduce_block, out, total):
    sum_steps(total, out, dot(hidden[0], reduce_block[:, 0].reshape(out.shape[1], -1), 1, 1))


def feed_sum(kernel, name, units, blocks, specs):
    tokens = units[0].shape[1]
    cycle, size, both, chunk = blocks.shape
    model = both // 3 * 2 * size
    unit = pl.BlockSpec((1, tokens, chunk), lambda j: (j, 0, 0))
    return pl.pallas_call(
        kernel,
        grid=(size,),
        in_specs=[unit] * len(units) + specs,
        out_specs=pl.BlockSpec((tokens, model), lambda j: (0, 0)),
        out_shape=jax.ShapeDtypeStruct((tokens, model), BF16),
        scratch_shapes=[pltpu.VMEM((tokens, model), F32)],
        compiler_params=pltpu.CompilerParams(vmem_limit_bytes=VMEM_LIMIT),
        cost_estimate=pl.CostEstimate(
            flops=2 * len(units) * tokens * model * size * chunk,
            bytes_accessed=2 * len(units) * (model + tokens) * size * chunk + 2 * tokens * model,
            transcendentals=0,
        ),
        name=name,
    )(*units, *[blocks] * len(specs))


def rotate(tensor, cosine, sine):
    half = HEAD // 2
    tokens = tensor.shape[1]
    split = tensor.reshape(-1, 2, half, tokens)
    first, second = (split[:, 0], split[:, 1])
    return jnp.stack(
        [first * cosine - second * sine, second * cosine + first * sine], axis=1
    ).reshape(-1, tokens)


def inverse_rms(stream):
    return lax.rsqrt(jnp.mean(stream * stream, axis=-1, keepdims=True) + EPS)


def norm_back(stream, gain, grad):
    scale = inverse_rms(stream)
    inner = jnp.mean(stream * gain * grad, axis=-1, keepdims=True)
    grad_stream = scale * (gain * grad) - stream * (scale * scale * scale * inner)
    return grad_stream, jnp.sum(grad * stream * scale, axis=0)


def adamw(weight, moment, variance, grad, rate, decay):
    moment = DECAY_FIRST * moment + (1.0 - DECAY_FIRST) * grad
    variance = DECAY_SECOND * variance + (1.0 - DECAY_SECOND) * grad * grad
    update = (
        moment
        / (1.0 - DECAY_FIRST**STEP)
        / (jnp.sqrt(variance / (1.0 - DECAY_SECOND**STEP)) + ADAM_EPS)
    )
    return (weight - rate * (update + decay * weight), moment, variance)


def adamw_kernel(weight, moment, variance, grad, *refs):
    new = adamw(
        weight[0], moment[0], variance[0], grad[...].astype(F32), RATE_MATRIX, WEIGHT_DECAY
    )
    for ref, value in zip(refs[-3:], new):
        ref[0] = value


def adamw_layer(state, grad, layer, earlier):
    rows, cols = grad.shape
    steps = 4 if rows % 64 == 0 else 1
    block = pl.BlockSpec((1, rows // steps, cols), lambda j: (layer, j, 0))
    held = pl.BlockSpec(memory_space=pl.ANY)
    shape = jax.ShapeDtypeStruct(state[0].shape, F32)
    return pl.pallas_call(
        adamw_kernel,
        grid=(steps,),
        in_specs=[block] * 3
        + [pl.BlockSpec((rows // steps, cols), lambda j: (j, 0))]
        + [held] * len(earlier),
        out_specs=[block] * 3,
        out_shape=[shape] * 3,
        input_output_aliases={4 + k: k for k in range(len(earlier))},
        compiler_params=pltpu.CompilerParams(vmem_limit_bytes=VMEM_LIMIT),
        cost_estimate=pl.CostEstimate(
            flops=20 * rows * cols, bytes_accessed=26 * rows * cols, transcendentals=2 * rows * cols
        ),
        name="adamw",
    )(*state, grad, *earlier)


def turned(arrays):
    return tuple(jnp.swapaxes(array, 1, 2) for array in arrays)


def body(
    block_in,
    cotangent,
    positions,
    attend_weight,
    attend_moment,
    attend_variance,
    output_weight,
    output_moment,
    output_variance,
    expand_weight,
    expand_moment,
    expand_variance,
    reduce_weight,
    reduce_moment,
    reduce_variance,
    gains,
    gains_moment,
    gains_variance,
):
    size = lax.axis_size("fsdp")
    cycle = lax.axis_size("ctx")
    row = lax.axis_index("fsdp")
    column = lax.axis_index("ctx")
    model = block_in.shape[2]
    att_rows, att_cols = attend_weight.shape[1:]
    out_rows, out_cols = output_weight.shape[1:]
    exp_rows, exp_cols = expand_weight.shape[1:]
    red_rows, red_cols = reduce_weight.shape[1:]
    chunk = exp_cols // size
    gain_cols = gains.shape[1]
    plane = column // 2
    by_half = attend_pairs(size, cycle)
    holds_values = column >= size + size // 2
    mixed_up = jnp.logical_and(column >= size, row % 2 == 1)
    half = att_cols // 2

    def send_attend(weight):
        low = weight.astype(BF16)
        lead, tail = exchange_attend(
            low[..., :half], low[..., half:], holds_values, mixed_up, by_half[0], by_half[1]
        )
        block = jnp.concatenate([lead, tail], axis=2)
        return jnp.concatenate([block, jnp.swapaxes(output_weight.astype(BF16), 1, 2)], axis=1)

    def exchange_rows(parts):
        return parts_from(exchange(parts_for(parts, row, size), "fsdp", 1, size), row)

    def send_feed(layer, *events):
        expand = expand_weight[layer].astype(BF16).reshape(exp_rows, size, chunk)
        reduce = reduce_weight[layer].astype(BF16).reshape(size, chunk, red_cols)
        parts = [jnp.transpose(expand, (1, 0, 2)), jnp.transpose(reduce, (0, 2, 1))]
        return exchange_rows(after(jnp.concatenate(parts, axis=1), *events))

    def gather(payload):
        return lax.all_gather(payload, "ctx", axis=0, tiled=False)

    pieces = []
    rest = gains
    for _ in range(GAIN_PARTS):
        part = rest.astype(BF16)
        rest = rest - part.astype(F32)
        pieces.append(part)
    gain_own = jnp.stack(pieces)
    gain_all = parts_from(exchange([gain_own] * size, "fsdp", 1, size), row)
    gain_flat = gain_all.reshape(-1, att_cols)
    gain_used = gain_flat.shape[0]

    tokens = block_in.shape[1]
    digits = jnp.stack([positions[0] // RUN, positions[0] % RUN], axis=1).astype(BF16)
    digits = jnp.pad(digits, ((0, 0), (0, LANES - digits.shape[1])))
    both = jnp.concatenate([block_in[0], digits, cotangent[0]], axis=1)
    both = parts_for(both.reshape(size, -1, both.shape[-1]), row, size)
    both, attend_first = lax.optimization_barrier((both, attend_weight))
    both = to_plane_rows(both, size, row)
    stream_low = to_plane(both[..., : model + LANES], size, plane)
    attend_sent = send_attend(attend_first)
    gain_rows = jnp.pad(gain_flat, ((0, GAIN_ROWS - gain_used), (0, 0)))
    payload = jnp.concatenate([attend_sent.reshape(-1, att_cols), gain_rows])
    payload, stream_low = lax.optimization_barrier((payload, stream_low))
    attn_parts = gather(payload)
    payload, both = lax.optimization_barrier((payload, both))
    payload = send_feed(0, payload)
    mlp_parts = [gather(payload)]
    back_low = to_plane(both[..., model + LANES :], size, plane)
    payload, stream_low = lax.optimization_barrier((payload, stream_low))
    stream_all = gather_tokens(stream_low, size)
    order = stream_all[:, model : model + 2].astype(jnp.int32)
    order = order[:, 0] * RUN + order[:, 1]
    order_far = swap_core(order, cycle)
    stream_first = stream_all[:, :model]
    stream_low = stream_low[:, :model]
    payload = send_feed(1, stream_all)
    mlp_parts.append(gather(payload))
    payload, back_low = lax.optimization_barrier((payload, back_low))
    back_all = gather_tokens(back_low, size)
    attn_rows = att_rows + out_cols
    gain_table = attn_parts[:, LAYERS * attn_rows : LAYERS * attn_rows + gain_used]
    gain_table = gain_table.reshape(cycle, size, GAIN_PARTS, 2 * LAYERS, gain_cols).astype(F32)
    gain_table = gain_table[:, :, 0] + gain_table[:, :, 1] + gain_table[:, :, 2]
    gain_table = jnp.transpose(gain_table, (2, 1, 0, 3)).reshape(2 * LAYERS, model)

    def attn_weights(layer):
        part = attn_parts[:, layer * attn_rows : (layer + 1) * attn_rows]
        block = part[:, :att_rows]
        return (
            block[:size].reshape(model, att_cols),
            block[size:].reshape(model, att_cols),
            part[:, att_rows:attn_rows].reshape(model, out_rows),
        )

    freq = THETA ** (-2.0 * jnp.arange(HEAD // 2, dtype=F32) / HEAD)
    angle = freq[:, None] * order.astype(F32)[None, :]
    cosine, sine = (jnp.cos(angle), jnp.sin(angle))

    stream = stream_low.astype(F32)
    stream_first = stream_first.astype(F32)
    saved = []
    for layer in range(LAYERS):
        gain_attend, gain_mix = (gain_table[2 * layer], gain_table[2 * layer + 1])
        query_weight, pair_weight, output_t = attn_weights(layer)
        if layer == 0:
            acts = (stream_first * inverse_rms(stream_first) * gain_attend).astype(BF16)
        else:
            acts = gather_tokens((stream * inverse_rms(stream) * gain_attend).astype(BF16), size)
        queries = rotate(dot(query_weight, acts, 0, 1), cosine, sine).astype(BF16)
        pair = dot(pair_weight, acts, 0, 1)
        pair = jnp.concatenate(
            [rotate(pair[: pair.shape[0] // 2], cosine, sine), pair[pair.shape[0] // 2 :]]
        ).astype(BF16)
        pair_far = swap_core(pair, cycle)
        mixed, totals = attend(queries, pair, pair_far, order, order_far)
        middle = stream + scatter_tokens(dot(mixed, output_t, 0, 1), size)
        middle_low = gather_tokens((middle * inverse_rms(middle) * gain_mix).astype(BF16), size)
        if layer == 0:
            mlp_parts[0] = after(mlp_parts[0], back_all)
        if layer == LAYERS - 1:
            hidden, grad_gate, grad_up, mlp_payload = feed_last(middle_low, back_all, mlp_parts[layer])
            gate, up = (None, None)
        else:
            gate, up, hidden, partial = feed(middle_low, mlp_parts[layer])
        if layer < LAYERS - 1:
            stream_next = middle + scatter_tokens(partial, size)
        saved.append((stream, acts, queries, pair, pair_far, mixed, totals, middle, middle_low, gate, up, hidden))
        stream = stream_next

    back = back_low.astype(F32)
    gain_grads = [None] * (2 * LAYERS)

    def reduce(payload):
        return lax.psum_scatter(payload, "ctx", scatter_dimension=0, tiled=False)

    mlp_grads = {}
    attn_payload = jnp.zeros((cycle, LAYERS * attn_rows + GAIN_ROWS, att_cols), BF16)

    for layer in reversed(range(LAYERS)):
        stream, acts, queries, pair, pair_far, mixed, totals, middle, middle_low, gate, up, hidden = saved[layer]
        gain_attend, gain_mix = (gain_table[2 * layer], gain_table[2 * layer + 1])
        query_weight, pair_weight, output_t = attn_weights(layer)
        if layer < LAYERS - 1:
            back_all = gather_tokens(back.astype(BF16), size)
            grad_gate, grad_up, mlp_payload = feed_turn(
                middle_low, back_all, hidden, gate, up, mlp_parts[layer]
            )
        else:
            last = (middle, hidden)
        mlp_grads[layer] = reduce(mlp_payload)
        grad_gate, mlp_payload = lax.optimization_barrier((grad_gate, mlp_payload))
        specs = block_specs(mlp_parts[layer])
        grad_partial = feed_sum(
            feed_input_kernel, "feed_input", [grad_gate, grad_up], mlp_parts[layer], specs[:2]
        )
        grad_middle = scatter_tokens(grad_partial, size)
        change, gain_grads[2 * layer + 1] = norm_back(middle, gain_mix, grad_middle)
        back = back + change
        back_attend = gather_tokens(back.astype(BF16), size)
        grad_mixed = dot(output_t, back_attend, 0, 1).astype(BF16)
        grad_query, key_own, key_far, value_own, value_far = attend_back(
            queries, grad_mixed, pair, pair_far, order, order_far, totals
        )
        from_far = swap_core(jnp.concatenate([key_far, value_far]).astype(BF16), cycle).astype(F32)
        rows_kv = key_own.shape[0]
        grad_key = key_own + from_far[:rows_kv]
        grad_value = value_own + from_far[rows_kv:]
        grad_query = rotate(grad_query.astype(BF16).astype(F32), cosine, -sine).astype(BF16)
        grad_key = rotate(grad_key.astype(BF16).astype(F32), cosine, -sine).astype(BF16)
        grad_pair = jnp.concatenate([grad_key, grad_value.astype(BF16)])
        grad_acts = dot(grad_query, query_weight, 0, 1) + dot(grad_pair, pair_weight, 0, 1)
        put = (LAYERS - 1 - layer) * attn_rows
        for first, value in ((0, dot(acts, grad_query, 0, 1)), (size, dot(acts, grad_pair, 0, 1))):
            value = value.astype(BF16).reshape(size, att_rows, att_cols)
            attn_payload = lax.dynamic_update_slice(attn_payload, value, (first, put, 0))
        value = dot(back_attend, mixed, 0, 1).astype(BF16).reshape(cycle, out_cols, out_rows)
        attn_payload = lax.dynamic_update_slice(attn_payload, value, (0, put + att_rows, 0))
        grad_stream = scatter_tokens(grad_acts, size)
        change, gain_grads[2 * layer] = norm_back(stream, gain_attend, grad_stream)
        back = back + change
        if layer == 0:
            gain_grads[0] = jnp.sum(grad_acts * stream_first * inverse_rms(stream_first), axis=0)
            table = jnp.stack(gain_grads).reshape(2 * LAYERS, size, cycle, gain_cols)
            table = jnp.transpose(table, (2, 1, 0, 3)).astype(BF16).reshape(cycle, -1, att_cols)
            attn_payload = lax.dynamic_update_slice(attn_payload, table, (0, LAYERS * attn_rows, 0))
        else:
            attn_payload, back = lax.optimization_barrier((attn_payload, back))

    states = {
        "attend": (attend_weight, attend_moment, attend_variance),
        "output": turned((output_weight, output_moment, output_variance)),
        "expand": (expand_weight, expand_moment, expand_variance),
        "reduce": turned((reduce_weight, reduce_moment, reduce_variance)),
    }
    renewed = {name: () for name in states}

    def renew(name, layer, grad):
        renewed[name] = adamw_layer(states[name], grad, layer, renewed[name])

    def renew_feed(layer, mlp_grad):
        mlp_grad = exchange_rows(mlp_grad)
        expand = jnp.transpose(mlp_grad[:, :exp_rows], (1, 0, 2)).reshape(exp_rows, exp_cols)
        reduce = jnp.transpose(mlp_grad[:, exp_rows:], (1, 0, 2)).reshape(red_cols, red_rows)
        renew("expand", layer, expand)
        renew("reduce", layer, reduce)

    def renew_attend(attn_grad):
        layers = attn_grad[: LAYERS * attn_rows].reshape(LAYERS, attn_rows, att_cols)
        block = layers[:, :att_rows]
        lead, tail = exchange_attend(
            block[..., :half],
            block[..., half:],
            mixed_up,
            holds_values,
            backwards(by_half[0]),
            backwards(by_half[1]),
        )
        block = jnp.concatenate([lead, tail], axis=2)
        for k, layer in enumerate(reversed(range(LAYERS))):
            renew("output", layer, layers[k, att_rows:])
            renew("attend", layer, block[k])

    attn_grad = reduce(attn_payload)
    for layer in reversed(range(1, LAYERS)):
        renew_feed(layer, after(mlp_grads[layer], attn_payload))
    block_out = feed_sum(
        feed_out_kernel, "feed_out", [after(last[1], attn_payload)], mlp_parts[-1], specs[2:]
    )
    block_out = last[0] + scatter_tokens(block_out, size)
    mlp_grads[0], renewed, block_out = lax.optimization_barrier((mlp_grads[0], renewed, block_out))
    renew_feed(0, mlp_grads[0])
    outs = jnp.concatenate([block_out, back], axis=1).astype(BF16)
    outs = from_plane(outs, size, row, plane)
    attn_grad, renewed, outs = lax.optimization_barrier((attn_grad, renewed, outs))
    renew_attend(attn_grad)
    grad_gains = attn_grad[LAYERS * attn_rows : LAYERS * attn_rows + table.shape[1]]
    grad_gains = grad_gains.astype(F32).reshape(size, 2 * LAYERS, gain_cols)
    grad_gains = sum(exchange(parts_for(grad_gains, row, size), "fsdp", 1, size))

    for name in ("output", "reduce"):
        renewed[name] = turned(renewed[name])
    results = [value for name in states for value in renewed[name]]
    results += list(adamw(gains, gains_moment, gains_variance, grad_gains, RATE_GAIN, 0.0))
    outs = outs.astype(F32)
    return (outs[None, :, :model], outs[None, :, model:], *results)


def solution(mesh):
    tokens = P("fsdp", "ctx", None)
    matrix = P(None, "fsdp", "ctx")
    gain = P(None, ("fsdp", "ctx"))
    return jax.shard_map(
        body,
        mesh=mesh,
        in_specs=(tokens, tokens, P("fsdp", "ctx")) + (matrix,) * 12 + (gain,) * 3,
        out_specs=(tokens, tokens) + (matrix,) * 12 + (gain,) * 3,
        check_vma=False,
    )
```

```python
import functools
import math

import jax
import jax.numpy as jnp
from jax import lax
from jax.experimental import pallas as pl
from jax.experimental.pallas import tpu as pltpu
from jax.sharding import PartitionSpec as P

HEADS = 16
KV_HEADS = 8
HEAD = 96
LAYERS = 2
STEP = 10

EPS = 1e-05
THETA = 100000.0
DECAY_FIRST = 0.9
DECAY_SECOND = 0.95
ADAM_EPS = 1e-08
WEIGHT_DECAY = 0.1
RATE_MATRIX = 0.06
RATE_GAIN = 0.6

BF16 = jnp.bfloat16
F32 = jnp.float32
SCALE = 1.0 / math.sqrt(HEAD)
GAIN_PARTS = 3
GAIN_ROWS = 16
RUN = 64
LANES = 128
BOTH = ("fsdp", "ctx")
VMEM_LIMIT = 60 * 1024 * 1024


def dot(left, right, contract_left, contract_right):
    return lax.dot_general(
        left,
        right,
        (((contract_left,), (contract_right,)), ((), ())),
        preferred_element_type=F32,
    )


def after(value, *events):
    return lax.optimization_barrier((value, *events))[0]


def swap(value, distance, size):
    return lax.ppermute(value, "fsdp", [(i, i ^ distance) for i in range(size)])


def swap_core(value, cycle):
    return lax.ppermute(value, "ctx", [(i, i ^ 1) for i in range(cycle)])


def exchange(parts, axis, step, size):
    cycle = lax.axis_size(axis)
    received = [parts[0]]
    for k in range(1, size):
        received.append(lax.ppermute(parts[k], axis, [(i, i ^ (k * step)) for i in range(cycle)]))
    return received


def parts_for(value, me, size):
    return [
        lax.dynamic_index_in_dim(value, jnp.bitwise_xor(me, k), 0, keepdims=False)
        for k in range(size)
    ]


def parts_from(parts, me):
    value = jnp.zeros((len(parts), *parts[0].shape), parts[0].dtype)
    for k, part in enumerate(parts):
        value = lax.dynamic_update_index_in_dim(value, part, jnp.bitwise_xor(me, k), 0)
    return value


def to_plane_rows(parts, size, row):
    return parts_from(exchange(parts, "fsdp", 1, size), row)


def to_plane(parts, size, plane):
    parts = exchange(parts_for(parts, plane, size), "ctx", 2, size)
    return jnp.concatenate(parts)


def from_plane(value, size):
    return exchange(value.reshape(size, -1, value.shape[-1]), "ctx", 2, size)


def from_plane_rows(parts, size, row, plane):
    parts = exchange(parts_for(parts_from(parts, plane), row, size), "fsdp", 1, size)
    value = parts_from(parts, row)
    return value.reshape(-1, value.shape[-1])


def attend_pairs(size, cycle):
    both = []
    for odd in range(2):
        pairs = []
        for row in range(size):
            for f in range(size):
                pairs.append((row * cycle + f, f * cycle + row))
            for k in range(size // 2):
                key_to, value_to = (2 * k + odd, 2 * k + 1 - odd)
                pairs.append((row * cycle + size + k, key_to * cycle + size + row))
                pairs.append((row * cycle + size + size // 2 + k, value_to * cycle + size + row))
        both.append(pairs)
    return both


def backwards(pairs):
    return [(target, source) for source, target in pairs]


def exchange_attend(first, second, flip_here, flip_there, pairs_first, pairs_second):
    lead = jnp.where(flip_here, second, first)
    tail = jnp.where(flip_here, first, second)
    lead = lax.ppermute(lead, BOTH, pairs_first)
    tail = lax.ppermute(tail, BOTH, pairs_second)
    return jnp.where(flip_there, tail, lead), jnp.where(flip_there, lead, tail)


def gather_tokens(piece, size):
    if size != 4:
        return jnp.concatenate([piece] + [swap(piece, k, size) for k in range(1, size)])
    half = piece.shape[0] // 2
    one = swap(piece, 1, size)
    two = swap(piece, 2, size)
    three_top = swap(one[:half], 2, size)
    three_low = swap(two[half:], 1, size)
    return jnp.concatenate([piece, one, two, three_top, three_low])


def scatter_tokens(partial, size):
    tokens = partial.shape[0] // size
    chunks = [partial[k * tokens : (k + 1) * tokens].astype(F32) for k in range(size)]
    if size != 4:
        total = chunks[0]
        for k in range(1, size):
            total = total + swap(chunks[k].astype(BF16), k, size).astype(F32)
        return total
    half = tokens // 2
    far = chunks[3].astype(BF16)
    via_one = swap(far[:half], 1, size).astype(F32)
    via_two = swap(far[half:], 2, size).astype(F32)
    one = jnp.concatenate([chunks[1][:half], chunks[1][half:] + via_two]).astype(BF16)
    two = jnp.concatenate([chunks[2][:half] + via_one, chunks[2][half:]]).astype(BF16)
    return chunks[0] + swap(one, 1, size).astype(F32) + swap(two, 2, size).astype(F32)


def attend_kernel(query, keys_own, keys_far, value_own, value_far, order, order_own, order_far, out, totals):
    queries = query[...]
    here = order[...]

    def scores(keys, key_order):
        block = dot(keys[...].T, queries, 1, 0) * SCALE
        return jnp.where(key_order[...] <= here, block, -1e30)

    own = scores(keys_own, order_own)
    far = scores(keys_far, order_far)
    top = jnp.maximum(jnp.max(own, axis=0, keepdims=True), jnp.max(far, axis=0, keepdims=True))
    own = jnp.exp(own - top)
    far = jnp.exp(far - top)
    total = jnp.sum(own, axis=0, keepdims=True) + jnp.sum(far, axis=0, keepdims=True)
    mixed = dot(value_own[...], own.astype(BF16), 1, 0) + dot(value_far[...], far.astype(BF16), 1, 0)
    out[...] = (mixed / total).astype(BF16)
    totals[0] = top + jnp.log(total)


def attend(queries, pair_own, pair_far, order, order_far):
    width, tokens = queries.shape
    kv_heads = pair_own.shape[0] // (2 * HEAD)
    group = width // HEAD // kv_heads
    head = lambda g, e: (g * group + e, 0)
    key = lambda g, e: (g, 0)
    value = lambda g, e: (kv_heads + g, 0)
    whole = lambda g, e: (0, 0)
    kv_block = (HEAD, tokens)
    return pl.pallas_call(
        attend_kernel,
        grid=(kv_heads, group),
        in_specs=[
            pl.BlockSpec((HEAD, tokens), head),
            pl.BlockSpec(kv_block, key),
            pl.BlockSpec(kv_block, key),
            pl.BlockSpec(kv_block, value),
            pl.BlockSpec(kv_block, value),
            pl.BlockSpec((1, tokens), whole),
            pl.BlockSpec((tokens, 1), whole),
            pl.BlockSpec((tokens, 1), whole),
        ],
        out_specs=[
            pl.BlockSpec((HEAD, tokens), head),
            pl.BlockSpec((1, 1, tokens), lambda g, e: (g * group + e, 0, 0)),
        ],
        out_shape=[
            jax.ShapeDtypeStruct((width, tokens), BF16),
            jax.ShapeDtypeStruct((width // HEAD, 1, tokens), F32),
        ],
        compiler_params=pltpu.CompilerParams(vmem_limit_bytes=56 * 1024 * 1024),
        cost_estimate=pl.CostEstimate(
            flops=8 * width * tokens * tokens,
            bytes_accessed=12 * width * tokens,
            transcendentals=2 * tokens * tokens * width // HEAD,
        ),
        name="attend",
    )(queries, pair_own, pair_far, pair_own, pair_far, order[None, :], order[:, None], order_far[:, None])


def attend_back_kernel(
    query, grad, keys_own, keys_far, value_own, value_far, order, order_own, order_far, totals,
    grad_query, grad_own, grad_far, grad_value_own, grad_value_far,
):
    queries = query[...]
    grads = grad[...]
    here = order[...]
    first = pl.program_id(1) == 0

    def terms(keys, values, key_order):
        block = dot(keys[...].T, queries, 1, 0) * SCALE
        block = jnp.where(key_order[...] <= here, block, -1e30)
        probs = jnp.exp(block - totals[0])
        return probs, dot(values[...].T, grads, 1, 0)

    probs_own, back_own = terms(keys_own, value_own, order_own)
    probs_far, back_far = terms(keys_far, value_far, order_far)
    delta = jnp.sum(probs_own * back_own, axis=0, keepdims=True) + jnp.sum(
        probs_far * back_far, axis=0, keepdims=True
    )
    score_own = (probs_own * (back_own - delta)).astype(BF16)
    score_far = (probs_far * (back_far - delta)).astype(BF16)
    grad_query[...] = (
        dot(keys_own[...], score_own, 1, 0) + dot(keys_far[...], score_far, 1, 0)
    ) * SCALE
    results = (
        (grad_own, dot(queries, score_own, 1, 1) * SCALE),
        (grad_far, dot(queries, score_far, 1, 1) * SCALE),
        (grad_value_own, dot(grads, probs_own.astype(BF16), 1, 1)),
        (grad_value_far, dot(grads, probs_far.astype(BF16), 1, 1)),
    )

    @pl.when(first)
    def _():
        for ref, value in results:
            ref[...] = value

    @pl.when(jnp.logical_not(first))
    def _():
        for ref, value in results:
            ref[...] += value


def attend_back(queries, grads, pair_own, pair_far, order, order_far, totals):
    width, tokens = queries.shape
    kv_heads = pair_own.shape[0] // (2 * HEAD)
    group = width // HEAD // kv_heads
    head = lambda g, e: (g * group + e, 0)
    key = lambda g, e: (g, 0)
    value = lambda g, e: (kv_heads + g, 0)
    whole = lambda g, e: (0, 0)
    block = (HEAD, tokens)
    kv_shape = jax.ShapeDtypeStruct((kv_heads * HEAD, tokens), F32)
    return pl.pallas_call(
        attend_back_kernel,
        grid=(kv_heads, group),
        in_specs=[
            pl.BlockSpec(block, head),
            pl.BlockSpec(block, head),
            pl.BlockSpec(block, key),
            pl.BlockSpec(block, key),
            pl.BlockSpec(block, value),
            pl.BlockSpec(block, value),
            pl.BlockSpec((1, tokens), whole),
            pl.BlockSpec((tokens, 1), whole),
            pl.BlockSpec((tokens, 1), whole),
            pl.BlockSpec((1, 1, tokens), lambda g, e: (g * group + e, 0, 0)),
        ],
        out_specs=[
            pl.BlockSpec(block, head),
            pl.BlockSpec(block, key),
            pl.BlockSpec(block, key),
            pl.BlockSpec(block, key),
            pl.BlockSpec(block, key),
        ],
        out_shape=[jax.ShapeDtypeStruct((width, tokens), F32)] + [kv_shape] * 4,
        compiler_params=pltpu.CompilerParams(vmem_limit_bytes=60 * 1024 * 1024),
        cost_estimate=pl.CostEstimate(
            flops=20 * width * tokens * tokens,
            bytes_accessed=24 * width * tokens,
            transcendentals=2 * tokens * tokens * width // HEAD,
        ),
        name="attend_back",
    )(
        queries, grads, pair_own, pair_far, pair_own, pair_far,
        order[None, :], order[:, None], order_far[:, None], totals,
    )


def swiglu_terms(gate):
    sigmoid = 1.0 / (1.0 + jnp.exp(-gate))
    return sigmoid, gate * sigmoid


def feed_kernel(acts, gate_block, up_block, reduce_block, gate_out, up_out, hidden_out, out, total):
    step = pl.program_id(0)
    model = acts.shape[1]
    gate = dot(acts[...], gate_block[0].reshape(model, -1), 1, 0)
    up = dot(acts[...], up_block[0].reshape(model, -1), 1, 0)
    hidden = (swiglu_terms(gate)[1] * up).astype(BF16)
    gate_out[0] = gate.astype(BF16)
    up_out[0] = up.astype(BF16)
    hidden_out[0] = hidden
    part = dot(hidden, reduce_block[:, 0].reshape(model, -1), 1, 1)

    @pl.when(step == 0)
    def _():
        total[...] = part

    @pl.when(step > 0)
    def _():
        total[...] += part

    @pl.when(step == pl.num_programs(0) - 1)
    def _():
        out[...] = total[...].astype(BF16)


def block_specs(blocks):
    cycle, size, both, chunk = blocks.shape
    rows = both // 3 * 2
    return [
        pl.BlockSpec((1, size, rows, chunk), lambda j: (j, 0, 0, 0)),
        pl.BlockSpec((1, size, rows, chunk), lambda j: (size + j, 0, 0, 0)),
        pl.BlockSpec((cycle, 1, both - rows, chunk), lambda j: (0, j, 2, 0)),
    ]


def feed(acts, blocks):
    tokens, model = acts.shape
    cycle, size, both, chunk = blocks.shape
    unit = pl.BlockSpec((1, tokens, chunk), lambda j: (j, 0, 0))
    whole = pl.BlockSpec((tokens, model), lambda j: (0, 0))
    units = jax.ShapeDtypeStruct((size, tokens, chunk), BF16)
    return pl.pallas_call(
        feed_kernel,
        grid=(size,),
        in_specs=[whole] + block_specs(blocks),
        out_specs=[unit, unit, unit, whole],
        out_shape=[units, units, units, jax.ShapeDtypeStruct((tokens, model), BF16)],
        scratch_shapes=[pltpu.VMEM((tokens, model), F32)],
        compiler_params=pltpu.CompilerParams(vmem_limit_bytes=VMEM_LIMIT),
        cost_estimate=pl.CostEstimate(
            flops=6 * tokens * model * size * chunk,
            bytes_accessed=2 * blocks.size + 4 * tokens * model + 6 * tokens * size * chunk,
            transcendentals=tokens * size * chunk,
        ),
        name="feed",
    )(acts, blocks, blocks, blocks)


def put_grads(out, units_buf, model_buf, sems, acts, grad, hidden, grad_gate, grad_up):
    step = pl.program_id(0)
    last = pl.num_programs(0) - 1
    slot = lax.rem(step, 2)
    cycle, size, both, chunk = out.shape
    rows = both // 3 * 2

    def copies(j, at):
        return (
            pltpu.make_async_copy(units_buf.at[at, 0], out.at[j, :, pl.ds(0, rows), :], sems.at[at, 0]),
            pltpu.make_async_copy(units_buf.at[at, 1], out.at[size + j, :, pl.ds(0, rows), :], sems.at[at, 1]),
            pltpu.make_async_copy(model_buf.at[at], out.at[:, j, pl.ds(rows, both - rows), :], sems.at[at, 2]),
        )

    @pl.when(step >= 2)
    def _():
        for copy in copies(step - 2, slot):
            copy.wait()

    units_buf[slot, 0] = dot(acts[...], grad_gate, 0, 0).astype(BF16).reshape(size, rows, chunk)
    units_buf[slot, 1] = dot(acts[...], grad_up, 0, 0).astype(BF16).reshape(size, rows, chunk)
    model_buf[slot] = dot(grad[...], hidden, 0, 0).astype(BF16).reshape(cycle, both - rows, chunk)
    for copy in copies(step, slot):
        copy.start()

    @pl.when(step == last)
    def _():
        for copy in copies(step - 1, 1 - slot):
            copy.wait()
        for copy in copies(step, slot):
            copy.wait()


def grads_scratch(shape):
    cycle, size, both, chunk = shape
    rows = both // 3 * 2
    return [
        pltpu.VMEM((2, 2, size, rows, chunk), BF16),
        pltpu.VMEM((2, cycle, both - rows, chunk), BF16),
        pltpu.SemaphoreType.DMA((2, 3)),
    ]


def feed_last_kernel(
    acts, grad, gate_block, up_block, reduce_block,
    hidden_out, grad_gate_out, grad_up_out, out, units_buf, model_buf, sems,
):
    model = acts.shape[1]
    gate = dot(acts[...], gate_block[0].reshape(model, -1), 1, 0)
    up = dot(acts[...], up_block[0].reshape(model, -1), 1, 0)
    grad_hidden = dot(grad[...], reduce_block[:, 0].reshape(model, -1), 1, 0)
    sigmoid, silu = swiglu_terms(gate)
    hidden = (silu * up).astype(BF16)
    grad_gate = (grad_hidden * up * (sigmoid + silu * (1.0 - sigmoid))).astype(BF16)
    grad_up = (grad_hidden * silu).astype(BF16)
    hidden_out[0] = hidden
    grad_gate_out[0] = grad_gate
    grad_up_out[0] = grad_up
    put_grads(out, units_buf, model_buf, sems, acts, grad, hidden, grad_gate, grad_up)


def feed_last(acts, grad, blocks):
    tokens, model = acts.shape
    cycle, size, both, chunk = blocks.shape
    unit = pl.BlockSpec((1, tokens, chunk), lambda j: (j, 0, 0))
    whole = pl.BlockSpec((tokens, model), lambda j: (0, 0))
    units = jax.ShapeDtypeStruct((size, tokens, chunk), BF16)
    return pl.pallas_call(
        feed_last_kernel,
        grid=(size,),
        in_specs=[whole, whole] + block_specs(blocks),
        out_specs=[unit, unit, unit, pl.BlockSpec(memory_space=pl.ANY)],
        out_shape=[units, units, units, jax.ShapeDtypeStruct(blocks.shape, BF16)],
        scratch_shapes=grads_scratch(blocks.shape),
        compiler_params=pltpu.CompilerParams(vmem_limit_bytes=VMEM_LIMIT),
        cost_estimate=pl.CostEstimate(
            flops=12 * tokens * model * size * chunk,
            bytes_accessed=4 * blocks.size + 4 * tokens * model + 6 * tokens * size * chunk,
            transcendentals=tokens * size * chunk,
        ),
        name="feed_last",
    )(acts, grad, blocks, blocks, blocks)


def feed_turn_kernel(
    acts, grad, hidden, gate_in, up_in, reduce_block,
    grad_gate_out, grad_up_out, out, units_buf, model_buf, sems,
):
    model = acts.shape[1]
    gate = gate_in[0].astype(F32)
    up = up_in[0].astype(F32)
    grad_hidden = dot(grad[...], reduce_block[:, 0].reshape(model, -1), 1, 0)
    sigmoid, silu = swiglu_terms(gate)
    grad_gate = (grad_hidden * up * (sigmoid + silu * (1.0 - sigmoid))).astype(BF16)
    grad_up = (grad_hidden * silu).astype(BF16)
    grad_gate_out[0] = grad_gate
    grad_up_out[0] = grad_up
    put_grads(out, units_buf, model_buf, sems, acts, grad, hidden[0], grad_gate, grad_up)


def feed_turn(acts, grad, hidden, gate, up, blocks):
    tokens, model = acts.shape
    cycle, size, both, chunk = blocks.shape
    unit = pl.BlockSpec((1, tokens, chunk), lambda j: (j, 0, 0))
    whole = pl.BlockSpec((tokens, model), lambda j: (0, 0))
    units = jax.ShapeDtypeStruct((size, tokens, chunk), BF16)
    return pl.pallas_call(
        feed_turn_kernel,
        grid=(size,),
        in_specs=[whole, whole, unit, unit, unit] + block_specs(blocks)[2:],
        out_specs=[unit, unit, pl.BlockSpec(memory_space=pl.ANY)],
        out_shape=[units, units, jax.ShapeDtypeStruct(blocks.shape, BF16)],
        scratch_shapes=grads_scratch(blocks.shape),
        compiler_params=pltpu.CompilerParams(vmem_limit_bytes=VMEM_LIMIT),
        cost_estimate=pl.CostEstimate(
            flops=8 * tokens * model * size * chunk,
            bytes_accessed=3 * blocks.size + 4 * tokens * model + 10 * tokens * size * chunk,
            transcendentals=tokens * size * chunk,
        ),
        name="feed_turn",
    )(acts, grad, hidden, gate, up, blocks)


def sum_steps(total, out, part):
    step = pl.program_id(0)

    @pl.when(step == 0)
    def _():
        total[...] = part

    @pl.when(step > 0)
    def _():
        total[...] += part

    @pl.when(step == pl.num_programs(0) - 1)
    def _():
        out[...] = total[...].astype(BF16)


def feed_input_kernel(grad_gate, grad_up, gate_block, up_block, out, total):
    model = out.shape[1]
    part = dot(grad_gate[0], gate_block[0].reshape(model, -1), 1, 1)
    part += dot(grad_up[0], up_block[0].reshape(model, -1), 1, 1)
    sum_steps(total, out, part)


def feed_out_kernel(hidden, reduce_block, out, total):
    sum_steps(total, out, dot(hidden[0], reduce_block[:, 0].reshape(out.shape[1], -1), 1, 1))


def feed_sum(kernel, name, units, blocks, specs):
    tokens = units[0].shape[1]
    cycle, size, both, chunk = blocks.shape
    model = both // 3 * 2 * size
    unit = pl.BlockSpec((1, tokens, chunk), lambda j: (j, 0, 0))
    return pl.pallas_call(
        kernel,
        grid=(size,),
        in_specs=[unit] * len(units) + specs,
        out_specs=pl.BlockSpec((tokens, model), lambda j: (0, 0)),
        out_shape=jax.ShapeDtypeStruct((tokens, model), BF16),
        scratch_shapes=[pltpu.VMEM((tokens, model), F32)],
        compiler_params=pltpu.CompilerParams(vmem_limit_bytes=VMEM_LIMIT),
        cost_estimate=pl.CostEstimate(
            flops=2 * len(units) * tokens * model * size * chunk,
            bytes_accessed=2 * len(units) * (model + tokens) * size * chunk + 2 * tokens * model,
            transcendentals=0,
        ),
        name=name,
    )(*units, *[blocks] * len(specs))


def rotate(tensor, cosine, sine):
    half = HEAD // 2
    tokens = tensor.shape[1]
    split = tensor.reshape(-1, 2, half, tokens)
    first, second = (split[:, 0], split[:, 1])
    return jnp.stack(
        [first * cosine - second * sine, second * cosine + first * sine], axis=1
    ).reshape(-1, tokens)


def inverse_rms(stream):
    return lax.rsqrt(jnp.mean(stream * stream, axis=-1, keepdims=True) + EPS)


def norm_back(stream, gain, grad):
    scale = inverse_rms(stream)
    inner = jnp.mean(stream * gain * grad, axis=-1, keepdims=True)
    grad_stream = scale * (gain * grad) - stream * (scale * scale * scale * inner)
    return grad_stream, jnp.sum(grad * stream * scale, axis=0)


def adamw(weight, moment, variance, grad, rate, decay):
    moment = DECAY_FIRST * moment + (1.0 - DECAY_FIRST) * grad
    variance = DECAY_SECOND * variance + (1.0 - DECAY_SECOND) * grad * grad
    update = (
        moment
        / (1.0 - DECAY_FIRST**STEP)
        / (jnp.sqrt(variance / (1.0 - DECAY_SECOND**STEP)) + ADAM_EPS)
    )
    return (weight - rate * (update + decay * weight), moment, variance)


def adamw_kernel(weight, moment, variance, grad, *refs):
    rows, cols = weight.shape[1:]
    value = grad[...].reshape(rows, cols).astype(F32)
    new = adamw(weight[0], moment[0], variance[0], value, RATE_MATRIX, WEIGHT_DECAY)
    for ref, value in zip(refs[-3:], new):
        ref[0] = value


def adamw_layer(state, grad, layer, earlier):
    rows, cols = grad.shape
    steps = 4 if rows % 64 == 0 else 1
    block = pl.BlockSpec((1, rows // steps, cols), lambda j: (layer, j, 0))
    held = pl.BlockSpec(memory_space=pl.ANY)
    shape = jax.ShapeDtypeStruct(state[0].shape, F32)
    return pl.pallas_call(
        adamw_kernel,
        grid=(steps,),
        in_specs=[block] * 3
        + [pl.BlockSpec((rows // steps, cols), lambda j: (j, 0))]
        + [held] * len(earlier),
        out_specs=[block] * 3,
        out_shape=[shape] * 3,
        input_output_aliases={4 + k: k for k in range(len(earlier))},
        compiler_params=pltpu.CompilerParams(vmem_limit_bytes=VMEM_LIMIT),
        cost_estimate=pl.CostEstimate(
            flops=20 * rows * cols, bytes_accessed=26 * rows * cols, transcendentals=2 * rows * cols
        ),
        name="adamw",
    )(*state, grad, *earlier)


def adamw_layers(state, grads):
    layers, rows, cols = grads.shape
    steps = 4 if rows % 64 == 0 else 1
    block = pl.BlockSpec((1, rows // steps, cols), lambda k, j: (k, j, 0))
    back = pl.BlockSpec((1, rows // steps, cols), lambda k, j: (layers - 1 - k, j, 0))
    return pl.pallas_call(
        adamw_kernel,
        grid=(layers, steps),
        in_specs=[block] * 3 + [back],
        out_specs=[block] * 3,
        out_shape=[jax.ShapeDtypeStruct(state[0].shape, F32)] * 3,
        compiler_params=pltpu.CompilerParams(vmem_limit_bytes=VMEM_LIMIT),
        cost_estimate=pl.CostEstimate(
            flops=20 * grads.size, bytes_accessed=26 * grads.size, transcendentals=2 * grads.size
        ),
        name="adamw",
    )(*state, grads)


def turned(arrays):
    return tuple(jnp.swapaxes(array, 1, 2) for array in arrays)


def body(
    block_in,
    cotangent,
    positions,
    attend_weight,
    attend_moment,
    attend_variance,
    output_weight,
    output_moment,
    output_variance,
    expand_weight,
    expand_moment,
    expand_variance,
    reduce_weight,
    reduce_moment,
    reduce_variance,
    gains,
    gains_moment,
    gains_variance,
):
    size = lax.axis_size("fsdp")
    cycle = lax.axis_size("ctx")
    row = lax.axis_index("fsdp")
    column = lax.axis_index("ctx")
    model = block_in.shape[2]
    att_rows, att_cols = attend_weight.shape[1:]
    out_rows, out_cols = output_weight.shape[1:]
    exp_rows, exp_cols = expand_weight.shape[1:]
    red_rows, red_cols = reduce_weight.shape[1:]
    chunk = exp_cols // size
    gain_cols = gains.shape[1]
    plane = column // 2
    by_half = attend_pairs(size, cycle)
    holds_values = column >= size + size // 2
    mixed_up = jnp.logical_and(column >= size, row % 2 == 1)
    half = att_cols // 2

    def send_attend(weight):
        low = weight.astype(BF16)
        lead, tail = exchange_attend(
            low[..., :half], low[..., half:], holds_values, mixed_up, by_half[0], by_half[1]
        )
        block = jnp.concatenate([lead, tail], axis=2)
        return jnp.concatenate([block, jnp.swapaxes(output_weight.astype(BF16), 1, 2)], axis=1)

    def exchange_rows(parts):
        return parts_from(exchange(parts_for(parts, row, size), "fsdp", 1, size), row)

    def send_feed(layer, *events):
        expand = expand_weight[layer].astype(BF16).reshape(exp_rows, size, chunk)
        reduce = reduce_weight[layer].astype(BF16).reshape(size, chunk, red_cols)
        parts = [jnp.transpose(expand, (1, 0, 2)), jnp.transpose(reduce, (0, 2, 1))]
        return exchange_rows(after(jnp.concatenate(parts, axis=1), *events))

    def gather(payload):
        return lax.all_gather(payload, "ctx", axis=0, tiled=False)

    pieces = []
    rest = gains
    for _ in range(GAIN_PARTS):
        part = rest.astype(BF16)
        rest = rest - part.astype(F32)
        pieces.append(part)
    gain_own = jnp.stack(pieces)
    gain_all = parts_from(exchange([gain_own] * size, "fsdp", 1, size), row)
    gain_flat = gain_all.reshape(-1, att_cols)
    gain_used = gain_flat.shape[0]

    tokens = block_in.shape[1]
    digits = jnp.stack([positions[0] // RUN, positions[0] % RUN], axis=1).astype(BF16)
    digits = jnp.pad(digits, ((0, 0), (0, LANES - digits.shape[1])))
    both = jnp.concatenate([block_in[0], digits, cotangent[0]], axis=1)
    both = parts_for(both.reshape(size, -1, both.shape[-1]), row, size)
    both, attend_first = lax.optimization_barrier((both, attend_weight))
    both = to_plane_rows(both, size, row)
    stream_low = to_plane(both[..., : model + LANES], size, plane)
    attend_sent = send_attend(attend_first)
    gain_rows = jnp.pad(gain_flat, ((0, GAIN_ROWS - gain_used), (0, 0)))
    payload = jnp.concatenate([attend_sent.reshape(-1, att_cols), gain_rows])
    payload, stream_low = lax.optimization_barrier((payload, stream_low))
    attn_parts = gather(payload)
    payload, both = lax.optimization_barrier((payload, both))
    payload = send_feed(0, payload)
    mlp_parts = [gather(payload)]
    back_low = to_plane(both[..., model + LANES :], size, plane)
    payload, stream_low = lax.optimization_barrier((payload, stream_low))
    stream_all = gather_tokens(stream_low, size)
    order = stream_all[:, model : model + 2].astype(jnp.int32)
    order = order[:, 0] * RUN + order[:, 1]
    order_far = swap_core(order, cycle)
    stream_first = stream_all[:, :model]
    stream_low = stream_low[:, :model]
    payload = send_feed(1, stream_all)
    mlp_parts.append(gather(payload))
    payload, back_low = lax.optimization_barrier((payload, back_low))
    back_all = gather_tokens(back_low, size)
    attn_rows = att_rows + out_cols
    gain_table = attn_parts[:, LAYERS * attn_rows : LAYERS * attn_rows + gain_used]
    gain_table = gain_table.reshape(cycle, size, GAIN_PARTS, 2 * LAYERS, gain_cols).astype(F32)
    gain_table = gain_table[:, :, 0] + gain_table[:, :, 1] + gain_table[:, :, 2]
    gain_table = jnp.transpose(gain_table, (2, 1, 0, 3)).reshape(2 * LAYERS, model)

    def attn_weights(layer):
        part = attn_parts[:, layer * attn_rows : (layer + 1) * attn_rows]
        block = part[:, :att_rows]
        return (
            block[:size].reshape(model, att_cols),
            block[size:].reshape(model, att_cols),
            part[:, att_rows:attn_rows].reshape(model, out_rows),
        )

    freq = THETA ** (-2.0 * jnp.arange(HEAD // 2, dtype=F32) / HEAD)
    angle = freq[:, None] * order.astype(F32)[None, :]
    cosine, sine = (jnp.cos(angle), jnp.sin(angle))

    stream = stream_low.astype(F32)
    stream_first = stream_first.astype(F32)
    saved = []
    for layer in range(LAYERS):
        gain_attend, gain_mix = (gain_table[2 * layer], gain_table[2 * layer + 1])
        query_weight, pair_weight, output_t = attn_weights(layer)
        if layer == 0:
            acts = (stream_first * inverse_rms(stream_first) * gain_attend).astype(BF16)
        else:
            acts = gather_tokens((stream * inverse_rms(stream) * gain_attend).astype(BF16), size)
        queries = rotate(dot(query_weight, acts, 0, 1), cosine, sine).astype(BF16)
        pair = dot(pair_weight, acts, 0, 1)
        pair = jnp.concatenate(
            [rotate(pair[: pair.shape[0] // 2], cosine, sine), pair[pair.shape[0] // 2 :]]
        ).astype(BF16)
        pair_far = swap_core(pair, cycle)
        mixed, totals = attend(queries, pair, pair_far, order, order_far)
        middle = stream + scatter_tokens(dot(mixed, output_t, 0, 1), size)
        middle_low = gather_tokens((middle * inverse_rms(middle) * gain_mix).astype(BF16), size)
        if layer == 0:
            mlp_parts[0] = after(mlp_parts[0], back_all)
        if layer == LAYERS - 1:
            hidden, grad_gate, grad_up, mlp_payload = feed_last(middle_low, back_all, mlp_parts[layer])
            gate, up = (None, None)
        else:
            gate, up, hidden, partial = feed(middle_low, mlp_parts[layer])
        if layer < LAYERS - 1:
            stream_next = middle + scatter_tokens(partial, size)
        saved.append((stream, acts, queries, pair, pair_far, mixed, totals, middle, middle_low, gate, up, hidden))
        stream = stream_next

    back = back_low.astype(F32)
    gain_grads = [None] * (2 * LAYERS)

    def reduce(payload):
        return lax.psum_scatter(payload, "ctx", scatter_dimension=0, tiled=False)

    mlp_grads = {}
    attn_grads = []

    for layer in reversed(range(LAYERS)):
        stream, acts, queries, pair, pair_far, mixed, totals, middle, middle_low, gate, up, hidden = saved[layer]
        gain_attend, gain_mix = (gain_table[2 * layer], gain_table[2 * layer + 1])
        query_weight, pair_weight, output_t = attn_weights(layer)
        if layer < LAYERS - 1:
            back_all = gather_tokens(back.astype(BF16), size)
            grad_gate, grad_up, mlp_payload = feed_turn(
                middle_low, back_all, hidden, gate, up, mlp_parts[layer]
            )
        else:
            last = (middle, hidden)
        mlp_grads[layer] = reduce(mlp_payload)
        grad_gate, mlp_payload = lax.optimization_barrier((grad_gate, mlp_payload))
        specs = block_specs(mlp_parts[layer])
        grad_partial = feed_sum(
            feed_input_kernel, "feed_input", [grad_gate, grad_up], mlp_parts[layer], specs[:2]
        )
        grad_middle = scatter_tokens(grad_partial, size)
        change, gain_grads[2 * layer + 1] = norm_back(middle, gain_mix, grad_middle)
        back = back + change
        back_attend = gather_tokens(back.astype(BF16), size)
        if layer == 0:
            early = after(mlp_grads[1], back_attend)
        grad_mixed = dot(output_t, back_attend, 0, 1).astype(BF16)
        grad_query, key_own, key_far, value_own, value_far = attend_back(
            queries, grad_mixed, pair, pair_far, order, order_far, totals
        )
        from_far = swap_core(jnp.concatenate([key_far, value_far]).astype(BF16), cycle).astype(F32)
        rows_kv = key_own.shape[0]
        grad_key = key_own + from_far[:rows_kv]
        grad_value = value_own + from_far[rows_kv:]
        grad_query = rotate(grad_query.astype(BF16).astype(F32), cosine, -sine).astype(BF16)
        grad_key = rotate(grad_key.astype(BF16).astype(F32), cosine, -sine).astype(BF16)
        grad_pair = jnp.concatenate([grad_key, grad_value.astype(BF16)])
        grad_acts = dot(grad_query, query_weight, 0, 1) + dot(grad_pair, pair_weight, 0, 1)
        parts = [
            jnp.concatenate([dot(acts, grad_query, 0, 1), dot(acts, grad_pair, 0, 1)])
            .astype(BF16)
            .reshape(cycle, att_rows, att_cols),
            dot(back_attend, mixed, 0, 1).astype(BF16).reshape(cycle, out_cols, out_rows),
        ]
        grad_stream = scatter_tokens(grad_acts, size)
        change, gain_grads[2 * layer] = norm_back(stream, gain_attend, grad_stream)
        back = back + change
        if layer == 0:
            gain_grads[0] = jnp.sum(grad_acts * stream_first * inverse_rms(stream_first), axis=0)
            table = jnp.stack(gain_grads).reshape(2 * LAYERS, size, cycle, gain_cols)
            table = jnp.transpose(table, (1, 2, 0, 3)).reshape(size, cycle, -1)
            table = sum(exchange(parts_for(table, row, size), "fsdp", 1, size))
            table = jnp.pad(table, ((0, 0), (0, att_cols - table.shape[1]))).astype(BF16)
            parts.append(jnp.pad(table[:, None], ((0, 0), (0, GAIN_ROWS - 1), (0, 0))))
        attn_payload = jnp.concatenate(parts, axis=1)
        if layer > 0:
            attn_payload, back = lax.optimization_barrier((attn_payload, back))
        attn_grads.append(reduce(attn_payload))

    states = {
        "attend": (attend_weight, attend_moment, attend_variance),
        "output": turned((output_weight, output_moment, output_variance)),
        "expand": (expand_weight, expand_moment, expand_variance),
        "reduce": turned((reduce_weight, reduce_moment, reduce_variance)),
    }
    renewed = {name: () for name in states}

    def renew(name, layer, grad):
        renewed[name] = adamw_layer(states[name], grad, layer, renewed[name])

    def renew_feed(layer, mlp_grad):
        expand = jnp.transpose(mlp_grad[:, :exp_rows], (1, 0, 2)).reshape(exp_rows, exp_cols)
        reduce = jnp.transpose(mlp_grad[:, exp_rows:], (1, 0, 2)).reshape(red_cols, red_rows)
        renew("expand", layer, expand)
        renew("reduce", layer, reduce)

    def renew_attend(attn_grads):
        block = jnp.stack([grad[:att_rows] for grad in attn_grads])
        lead, tail = exchange_attend(
            block[..., :half],
            block[..., half:],
            mixed_up,
            holds_values,
            backwards(by_half[0]),
            backwards(by_half[1]),
        )
        output = jnp.stack([grad[att_rows:attn_rows] for grad in attn_grads])
        renewed["output"] = adamw_layers(states["output"], output)
        renewed["attend"] = adamw_layers(states["attend"], jnp.concatenate([lead, tail], axis=2))

    sent_last = exchange_rows(early)
    block_out = feed_sum(
        feed_out_kernel, "feed_out", [after(last[1], attn_payload)], mlp_parts[-1], specs[2:]
    )
    block_out = last[0] + scatter_tokens(block_out, size)
    mlp_grads[0], sent_last, block_out = lax.optimization_barrier(
        (mlp_grads[0], sent_last, block_out)
    )
    sent = exchange_rows(mlp_grads[0])
    outs = from_plane(jnp.concatenate([block_out, back], axis=1).astype(BF16), size)
    attn_grads[-1], outs, sent = lax.optimization_barrier((attn_grads[-1], outs, sent))
    renew_attend(attn_grads)
    renew_feed(1, sent_last)
    renew_feed(0, sent)
    outs = from_plane_rows(outs, size, row, plane)
    grad_gains = attn_grads[-1][attn_rows, : 2 * LAYERS * gain_cols]
    grad_gains = grad_gains.astype(F32).reshape(2 * LAYERS, gain_cols)
    for name in ("output", "reduce"):
        renewed[name] = turned(renewed[name])
    results = [value for name in states for value in renewed[name]]
    results += list(adamw(gains, gains_moment, gains_variance, grad_gains, RATE_GAIN, 0.0))
    outs = outs.astype(F32)
    return (outs[None, :, :model], outs[None, :, model:], *results)


def solution(mesh):
    tokens = P("fsdp", "ctx", None)
    matrix = P(None, "fsdp", "ctx")
    gain = P(None, ("fsdp", "ctx"))
    return jax.shard_map(
        body,
        mesh=mesh,
        in_specs=(tokens, tokens, P("fsdp", "ctx")) + (matrix,) * 12 + (gain,) * 3,
        out_specs=(tokens, tokens) + (matrix,) * 12 + (gain,) * 3,
        check_vma=False,
    )
```

```python
import functools
import math

import jax
import jax.numpy as jnp
from jax import lax
from jax.experimental import pallas as pl
from jax.experimental.pallas import tpu as pltpu
from jax.sharding import PartitionSpec as P

HEADS = 16
KV_HEADS = 8
HEAD = 96
LAYERS = 2
STEP = 10

EPS = 1e-05
THETA = 100000.0
DECAY_FIRST = 0.9
DECAY_SECOND = 0.95
ADAM_EPS = 1e-08
WEIGHT_DECAY = 0.1
RATE_MATRIX = 0.06
RATE_GAIN = 0.6

BF16 = jnp.bfloat16
F32 = jnp.float32
SCALE = 1.0 / math.sqrt(HEAD)
GAIN_PARTS = 3
GAIN_ROWS = 16
RUN = 64
LANES = 128
BOTH = ("fsdp", "ctx")
VMEM_LIMIT = 60 * 1024 * 1024


def dot(left, right, contract_left, contract_right):
    return lax.dot_general(
        left,
        right,
        (((contract_left,), (contract_right,)), ((), ())),
        preferred_element_type=F32,
    )


def after(value, *events):
    return lax.optimization_barrier((value, *events))[0]


def swap(value, distance, size):
    return lax.ppermute(value, "fsdp", [(i, i ^ distance) for i in range(size)])


def swap_core(value, cycle):
    return lax.ppermute(value, "ctx", [(i, i ^ 1) for i in range(cycle)])


def exchange(parts, axis, step, size):
    cycle = lax.axis_size(axis)
    received = [parts[0]]
    for k in range(1, size):
        received.append(lax.ppermute(parts[k], axis, [(i, i ^ (k * step)) for i in range(cycle)]))
    return received


def parts_for(value, me, size):
    return [
        lax.dynamic_index_in_dim(value, jnp.bitwise_xor(me, k), 0, keepdims=False)
        for k in range(size)
    ]


def parts_from(parts, me):
    value = jnp.zeros((len(parts), *parts[0].shape), parts[0].dtype)
    for k, part in enumerate(parts):
        value = lax.dynamic_update_index_in_dim(value, part, jnp.bitwise_xor(me, k), 0)
    return value


def to_plane_rows(parts, size, row):
    return parts_from(exchange(parts, "fsdp", 1, size), row)


def to_plane(parts, size, plane):
    parts = exchange(parts_for(parts, plane, size), "ctx", 2, size)
    return jnp.concatenate(parts)


def from_plane(value, size):
    return exchange(value.reshape(size, -1, value.shape[-1]), "ctx", 2, size)


def from_plane_rows(parts, size, row, plane):
    parts = exchange(parts_for(parts_from(parts, plane), row, size), "fsdp", 1, size)
    value = parts_from(parts, row)
    return value.reshape(-1, value.shape[-1])


def attend_pairs(size, cycle):
    both = []
    for odd in range(2):
        pairs = []
        for row in range(size):
            for f in range(size):
                pairs.append((row * cycle + f, f * cycle + row))
            for k in range(size // 2):
                key_to, value_to = (2 * k + odd, 2 * k + 1 - odd)
                pairs.append((row * cycle + size + k, key_to * cycle + size + row))
                pairs.append((row * cycle + size + size // 2 + k, value_to * cycle + size + row))
        both.append(pairs)
    return both


def backwards(pairs):
    return [(target, source) for source, target in pairs]


def exchange_attend(first, second, flip_here, flip_there, pairs_first, pairs_second):
    lead = jnp.where(flip_here, second, first)
    tail = jnp.where(flip_here, first, second)
    lead = lax.ppermute(lead, BOTH, pairs_first)
    tail = lax.ppermute(tail, BOTH, pairs_second)
    return jnp.where(flip_there, tail, lead), jnp.where(flip_there, lead, tail)


def gather_tokens(piece, size):
    if size != 4:
        return jnp.concatenate([piece] + [swap(piece, k, size) for k in range(1, size)])
    half = piece.shape[0] // 2
    one = swap(piece, 1, size)
    two = swap(piece, 2, size)
    three_top = swap(one[:half], 2, size)
    three_low = swap(two[half:], 1, size)
    return jnp.concatenate([piece, one, two, three_top, three_low])


def scatter_tokens(partial, size):
    tokens = partial.shape[0] // size
    chunks = [partial[k * tokens : (k + 1) * tokens].astype(F32) for k in range(size)]
    if size != 4:
        total = chunks[0]
        for k in range(1, size):
            total = total + swap(chunks[k].astype(BF16), k, size).astype(F32)
        return total
    half = tokens // 2
    far = chunks[3].astype(BF16)
    via_one = swap(far[:half], 1, size).astype(F32)
    via_two = swap(far[half:], 2, size).astype(F32)
    one = jnp.concatenate([chunks[1][:half], chunks[1][half:] + via_two]).astype(BF16)
    two = jnp.concatenate([chunks[2][:half] + via_one, chunks[2][half:]]).astype(BF16)
    return chunks[0] + swap(one, 1, size).astype(F32) + swap(two, 2, size).astype(F32)


def attend_kernel(query, keys_own, keys_far, value_own, value_far, order, order_own, order_far, out, totals):
    queries = query[...]
    here = order[...]

    def scores(keys, key_order):
        block = dot(keys[...].T, queries, 1, 0) * SCALE
        return jnp.where(key_order[...] <= here, block, -1e30)

    own = scores(keys_own, order_own)
    far = scores(keys_far, order_far)
    top = jnp.maximum(jnp.max(own, axis=0, keepdims=True), jnp.max(far, axis=0, keepdims=True))
    own = jnp.exp(own - top)
    far = jnp.exp(far - top)
    total = jnp.sum(own, axis=0, keepdims=True) + jnp.sum(far, axis=0, keepdims=True)
    mixed = dot(value_own[...], own.astype(BF16), 1, 0) + dot(value_far[...], far.astype(BF16), 1, 0)
    out[...] = (mixed / total).astype(BF16)
    totals[0] = top + jnp.log(total)


def attend(queries, pair_own, pair_far, order, order_far):
    width, tokens = queries.shape
    kv_heads = pair_own.shape[0] // (2 * HEAD)
    group = width // HEAD // kv_heads
    head = lambda g, e: (g * group + e, 0)
    key = lambda g, e: (g, 0)
    value = lambda g, e: (kv_heads + g, 0)
    whole = lambda g, e: (0, 0)
    kv_block = (HEAD, tokens)
    return pl.pallas_call(
        attend_kernel,
        grid=(kv_heads, group),
        in_specs=[
            pl.BlockSpec((HEAD, tokens), head),
            pl.BlockSpec(kv_block, key),
            pl.BlockSpec(kv_block, key),
            pl.BlockSpec(kv_block, value),
            pl.BlockSpec(kv_block, value),
            pl.BlockSpec((1, tokens), whole),
            pl.BlockSpec((tokens, 1), whole),
            pl.BlockSpec((tokens, 1), whole),
        ],
        out_specs=[
            pl.BlockSpec((HEAD, tokens), head),
            pl.BlockSpec((1, 1, tokens), lambda g, e: (g * group + e, 0, 0)),
        ],
        out_shape=[
            jax.ShapeDtypeStruct((width, tokens), BF16),
            jax.ShapeDtypeStruct((width // HEAD, 1, tokens), F32),
        ],
        compiler_params=pltpu.CompilerParams(vmem_limit_bytes=56 * 1024 * 1024),
        cost_estimate=pl.CostEstimate(
            flops=8 * width * tokens * tokens,
            bytes_accessed=12 * width * tokens,
            transcendentals=2 * tokens * tokens * width // HEAD,
        ),
        name="attend",
    )(queries, pair_own, pair_far, pair_own, pair_far, order[None, :], order[:, None], order_far[:, None])


def attend_back_kernel(
    query, grad, keys_own, keys_far, value_own, value_far, order, order_own, order_far, totals,
    grad_query, grad_own, grad_far, grad_value_own, grad_value_far,
):
    queries = query[...]
    grads = grad[...]
    here = order[...]
    first = pl.program_id(1) == 0

    def terms(keys, values, key_order):
        block = dot(keys[...].T, queries, 1, 0) * SCALE
        block = jnp.where(key_order[...] <= here, block, -1e30)
        probs = jnp.exp(block - totals[0])
        return probs, dot(values[...].T, grads, 1, 0)

    probs_own, back_own = terms(keys_own, value_own, order_own)
    probs_far, back_far = terms(keys_far, value_far, order_far)
    delta = jnp.sum(probs_own * back_own, axis=0, keepdims=True) + jnp.sum(
        probs_far * back_far, axis=0, keepdims=True
    )
    score_own = (probs_own * (back_own - delta)).astype(BF16)
    score_far = (probs_far * (back_far - delta)).astype(BF16)
    grad_query[...] = (
        dot(keys_own[...], score_own, 1, 0) + dot(keys_far[...], score_far, 1, 0)
    ) * SCALE
    results = (
        (grad_own, dot(queries, score_own, 1, 1) * SCALE),
        (grad_far, dot(queries, score_far, 1, 1) * SCALE),
        (grad_value_own, dot(grads, probs_own.astype(BF16), 1, 1)),
        (grad_value_far, dot(grads, probs_far.astype(BF16), 1, 1)),
    )

    @pl.when(first)
    def _():
        for ref, value in results:
            ref[...] = value

    @pl.when(jnp.logical_not(first))
    def _():
        for ref, value in results:
            ref[...] += value


def attend_back(queries, grads, pair_own, pair_far, order, order_far, totals):
    width, tokens = queries.shape
    kv_heads = pair_own.shape[0] // (2 * HEAD)
    group = width // HEAD // kv_heads
    head = lambda g, e: (g * group + e, 0)
    key = lambda g, e: (g, 0)
    value = lambda g, e: (kv_heads + g, 0)
    whole = lambda g, e: (0, 0)
    block = (HEAD, tokens)
    kv_shape = jax.ShapeDtypeStruct((kv_heads * HEAD, tokens), F32)
    return pl.pallas_call(
        attend_back_kernel,
        grid=(kv_heads, group),
        in_specs=[
            pl.BlockSpec(block, head),
            pl.BlockSpec(block, head),
            pl.BlockSpec(block, key),
            pl.BlockSpec(block, key),
            pl.BlockSpec(block, value),
            pl.BlockSpec(block, value),
            pl.BlockSpec((1, tokens), whole),
            pl.BlockSpec((tokens, 1), whole),
            pl.BlockSpec((tokens, 1), whole),
            pl.BlockSpec((1, 1, tokens), lambda g, e: (g * group + e, 0, 0)),
        ],
        out_specs=[
            pl.BlockSpec(block, head),
            pl.BlockSpec(block, key),
            pl.BlockSpec(block, key),
            pl.BlockSpec(block, key),
            pl.BlockSpec(block, key),
        ],
        out_shape=[jax.ShapeDtypeStruct((width, tokens), F32)] + [kv_shape] * 4,
        compiler_params=pltpu.CompilerParams(vmem_limit_bytes=60 * 1024 * 1024),
        cost_estimate=pl.CostEstimate(
            flops=20 * width * tokens * tokens,
            bytes_accessed=24 * width * tokens,
            transcendentals=2 * tokens * tokens * width // HEAD,
        ),
        name="attend_back",
    )(
        queries, grads, pair_own, pair_far, pair_own, pair_far,
        order[None, :], order[:, None], order_far[:, None], totals,
    )


def swiglu_terms(gate):
    sigmoid = 1.0 / (1.0 + jnp.exp(-gate))
    return sigmoid, gate * sigmoid


def feed_kernel(acts, gate_block, up_block, reduce_block, gate_out, up_out, hidden_out, out, total):
    step = pl.program_id(0)
    model = acts.shape[1]
    gate = dot(acts[...], gate_block[0].reshape(model, -1), 1, 0)
    up = dot(acts[...], up_block[0].reshape(model, -1), 1, 0)
    hidden = (swiglu_terms(gate)[1] * up).astype(BF16)
    gate_out[0] = gate.astype(BF16)
    up_out[0] = up.astype(BF16)
    hidden_out[0] = hidden
    part = dot(hidden, reduce_block[:, 0].reshape(model, -1), 1, 1)

    @pl.when(step == 0)
    def _():
        total[...] = part

    @pl.when(step > 0)
    def _():
        total[...] += part

    @pl.when(step == pl.num_programs(0) - 1)
    def _():
        out[...] = total[...].astype(BF16)


def block_specs(blocks):
    cycle, size, both, chunk = blocks.shape
    rows = both // 3 * 2
    return [
        pl.BlockSpec((1, size, rows, chunk), lambda j: (j, 0, 0, 0)),
        pl.BlockSpec((1, size, rows, chunk), lambda j: (size + j, 0, 0, 0)),
        pl.BlockSpec((cycle, 1, both - rows, chunk), lambda j: (0, j, 2, 0)),
    ]


def feed(acts, blocks):
    tokens, model = acts.shape
    cycle, size, both, chunk = blocks.shape
    unit = pl.BlockSpec((1, tokens, chunk), lambda j: (j, 0, 0))
    whole = pl.BlockSpec((tokens, model), lambda j: (0, 0))
    units = jax.ShapeDtypeStruct((size, tokens, chunk), BF16)
    return pl.pallas_call(
        feed_kernel,
        grid=(size,),
        in_specs=[whole] + block_specs(blocks),
        out_specs=[unit, unit, unit, whole],
        out_shape=[units, units, units, jax.ShapeDtypeStruct((tokens, model), BF16)],
        scratch_shapes=[pltpu.VMEM((tokens, model), F32)],
        compiler_params=pltpu.CompilerParams(vmem_limit_bytes=VMEM_LIMIT),
        cost_estimate=pl.CostEstimate(
            flops=6 * tokens * model * size * chunk,
            bytes_accessed=2 * blocks.size + 4 * tokens * model + 6 * tokens * size * chunk,
            transcendentals=tokens * size * chunk,
        ),
        name="feed",
    )(acts, blocks, blocks, blocks)


def put_grads(out, units_buf, model_buf, sems, acts, grad, hidden, grad_gate, grad_up):
    step = pl.program_id(0)
    last = pl.num_programs(0) - 1
    slot = lax.rem(step, 2)
    cycle, size, both, chunk = out.shape
    rows = both // 3 * 2

    def copies(j, at):
        return (
            pltpu.make_async_copy(units_buf.at[at, 0], out.at[j, :, pl.ds(0, rows), :], sems.at[at, 0]),
            pltpu.make_async_copy(units_buf.at[at, 1], out.at[size + j, :, pl.ds(0, rows), :], sems.at[at, 1]),
            pltpu.make_async_copy(model_buf.at[at], out.at[:, j, pl.ds(rows, both - rows), :], sems.at[at, 2]),
        )

    @pl.when(step >= 2)
    def _():
        for copy in copies(step - 2, slot):
            copy.wait()

    units_buf[slot, 0] = dot(acts[...], grad_gate, 0, 0).astype(BF16).reshape(size, rows, chunk)
    units_buf[slot, 1] = dot(acts[...], grad_up, 0, 0).astype(BF16).reshape(size, rows, chunk)
    model_buf[slot] = dot(grad[...], hidden, 0, 0).astype(BF16).reshape(cycle, both - rows, chunk)
    for copy in copies(step, slot):
        copy.start()

    @pl.when(step == last)
    def _():
        for copy in copies(step - 1, 1 - slot):
            copy.wait()
        for copy in copies(step, slot):
            copy.wait()


def grads_scratch(shape):
    cycle, size, both, chunk = shape
    rows = both // 3 * 2
    return [
        pltpu.VMEM((2, 2, size, rows, chunk), BF16),
        pltpu.VMEM((2, cycle, both - rows, chunk), BF16),
        pltpu.SemaphoreType.DMA((2, 3)),
    ]


def feed_last_kernel(
    acts, grad, gate_block, up_block, reduce_block,
    hidden_out, grad_gate_out, grad_up_out, out, units_buf, model_buf, sems,
):
    model = acts.shape[1]
    gate = dot(acts[...], gate_block[0].reshape(model, -1), 1, 0)
    up = dot(acts[...], up_block[0].reshape(model, -1), 1, 0)
    grad_hidden = dot(grad[...], reduce_block[:, 0].reshape(model, -1), 1, 0)
    sigmoid, silu = swiglu_terms(gate)
    hidden = (silu * up).astype(BF16)
    grad_gate = (grad_hidden * up * (sigmoid + silu * (1.0 - sigmoid))).astype(BF16)
    grad_up = (grad_hidden * silu).astype(BF16)
    hidden_out[0] = hidden
    grad_gate_out[0] = grad_gate
    grad_up_out[0] = grad_up
    put_grads(out, units_buf, model_buf, sems, acts, grad, hidden, grad_gate, grad_up)


def feed_last(acts, grad, blocks):
    tokens, model = acts.shape
    cycle, size, both, chunk = blocks.shape
    unit = pl.BlockSpec((1, tokens, chunk), lambda j: (j, 0, 0))
    whole = pl.BlockSpec((tokens, model), lambda j: (0, 0))
    units = jax.ShapeDtypeStruct((size, tokens, chunk), BF16)
    return pl.pallas_call(
        feed_last_kernel,
        grid=(size,),
        in_specs=[whole, whole] + block_specs(blocks),
        out_specs=[unit, unit, unit, pl.BlockSpec(memory_space=pl.ANY)],
        out_shape=[units, units, units, jax.ShapeDtypeStruct(blocks.shape, BF16)],
        scratch_shapes=grads_scratch(blocks.shape),
        compiler_params=pltpu.CompilerParams(vmem_limit_bytes=VMEM_LIMIT),
        cost_estimate=pl.CostEstimate(
            flops=12 * tokens * model * size * chunk,
            bytes_accessed=4 * blocks.size + 4 * tokens * model + 6 * tokens * size * chunk,
            transcendentals=tokens * size * chunk,
        ),
        name="feed_last",
    )(acts, grad, blocks, blocks, blocks)


def feed_turn_kernel(
    acts, grad, hidden, gate_in, up_in, reduce_block,
    grad_gate_out, grad_up_out, out, units_buf, model_buf, sems,
):
    model = acts.shape[1]
    gate = gate_in[0].astype(F32)
    up = up_in[0].astype(F32)
    grad_hidden = dot(grad[...], reduce_block[:, 0].reshape(model, -1), 1, 0)
    sigmoid, silu = swiglu_terms(gate)
    grad_gate = (grad_hidden * up * (sigmoid + silu * (1.0 - sigmoid))).astype(BF16)
    grad_up = (grad_hidden * silu).astype(BF16)
    grad_gate_out[0] = grad_gate
    grad_up_out[0] = grad_up
    put_grads(out, units_buf, model_buf, sems, acts, grad, hidden[0], grad_gate, grad_up)


def feed_turn(acts, grad, hidden, gate, up, blocks):
    tokens, model = acts.shape
    cycle, size, both, chunk = blocks.shape
    unit = pl.BlockSpec((1, tokens, chunk), lambda j: (j, 0, 0))
    whole = pl.BlockSpec((tokens, model), lambda j: (0, 0))
    units = jax.ShapeDtypeStruct((size, tokens, chunk), BF16)
    return pl.pallas_call(
        feed_turn_kernel,
        grid=(size,),
        in_specs=[whole, whole, unit, unit, unit] + block_specs(blocks)[2:],
        out_specs=[unit, unit, pl.BlockSpec(memory_space=pl.ANY)],
        out_shape=[units, units, jax.ShapeDtypeStruct(blocks.shape, BF16)],
        scratch_shapes=grads_scratch(blocks.shape),
        compiler_params=pltpu.CompilerParams(vmem_limit_bytes=VMEM_LIMIT),
        cost_estimate=pl.CostEstimate(
            flops=8 * tokens * model * size * chunk,
            bytes_accessed=3 * blocks.size + 4 * tokens * model + 10 * tokens * size * chunk,
            transcendentals=tokens * size * chunk,
        ),
        name="feed_turn",
    )(acts, grad, hidden, gate, up, blocks)


def sum_steps(total, out, part):
    step = pl.program_id(0)

    @pl.when(step == 0)
    def _():
        total[...] = part

    @pl.when(step > 0)
    def _():
        total[...] += part

    @pl.when(step == pl.num_programs(0) - 1)
    def _():
        out[...] = total[...].astype(BF16)


def feed_input_kernel(grad_gate, grad_up, gate_block, up_block, out, total):
    model = out.shape[1]
    part = dot(grad_gate[0], gate_block[0].reshape(model, -1), 1, 1)
    part += dot(grad_up[0], up_block[0].reshape(model, -1), 1, 1)
    sum_steps(total, out, part)


def feed_out_kernel(hidden, reduce_block, out, total):
    sum_steps(total, out, dot(hidden[0], reduce_block[:, 0].reshape(out.shape[1], -1), 1, 1))


def feed_sum(kernel, name, units, blocks, specs):
    tokens = units[0].shape[1]
    cycle, size, both, chunk = blocks.shape
    model = both // 3 * 2 * size
    unit = pl.BlockSpec((1, tokens, chunk), lambda j: (j, 0, 0))
    return pl.pallas_call(
        kernel,
        grid=(size,),
        in_specs=[unit] * len(units) + specs,
        out_specs=pl.BlockSpec((tokens, model), lambda j: (0, 0)),
        out_shape=jax.ShapeDtypeStruct((tokens, model), BF16),
        scratch_shapes=[pltpu.VMEM((tokens, model), F32)],
        compiler_params=pltpu.CompilerParams(vmem_limit_bytes=VMEM_LIMIT),
        cost_estimate=pl.CostEstimate(
            flops=2 * len(units) * tokens * model * size * chunk,
            bytes_accessed=2 * len(units) * (model + tokens) * size * chunk + 2 * tokens * model,
            transcendentals=0,
        ),
        name=name,
    )(*units, *[blocks] * len(specs))


def rotate(tensor, cosine, sine):
    half = HEAD // 2
    tokens = tensor.shape[1]
    split = tensor.reshape(-1, 2, half, tokens)
    first, second = (split[:, 0], split[:, 1])
    return jnp.stack(
        [first * cosine - second * sine, second * cosine + first * sine], axis=1
    ).reshape(-1, tokens)


def inverse_rms(stream):
    return lax.rsqrt(jnp.mean(stream * stream, axis=-1, keepdims=True) + EPS)


def norm_back(stream, gain, grad):
    scale = inverse_rms(stream)
    inner = jnp.mean(stream * gain * grad, axis=-1, keepdims=True)
    grad_stream = scale * (gain * grad) - stream * (scale * scale * scale * inner)
    return grad_stream, jnp.sum(grad * stream * scale, axis=0)


def adamw(weight, moment, variance, grad, rate, decay):
    moment = DECAY_FIRST * moment + (1.0 - DECAY_FIRST) * grad
    variance = DECAY_SECOND * variance + (1.0 - DECAY_SECOND) * grad * grad
    update = (
        moment
        / (1.0 - DECAY_FIRST**STEP)
        / (jnp.sqrt(variance / (1.0 - DECAY_SECOND**STEP)) + ADAM_EPS)
    )
    return (weight - rate * (update + decay * weight), moment, variance)


def adamw_kernel(weight, moment, variance, grad, *refs):
    rows, cols = weight.shape[1:]
    value = grad[...].reshape(rows, cols).astype(F32)
    new = adamw(weight[0], moment[0], variance[0], value, RATE_MATRIX, WEIGHT_DECAY)
    for ref, value in zip(refs[-3:], new):
        ref[0] = value


def adamw_layer(state, grad, layer, earlier):
    rows, cols = grad.shape
    steps = 4 if rows % 64 == 0 else 1
    block = pl.BlockSpec((1, rows // steps, cols), lambda j: (layer, j, 0))
    held = pl.BlockSpec(memory_space=pl.ANY)
    shape = jax.ShapeDtypeStruct(state[0].shape, F32)
    return pl.pallas_call(
        adamw_kernel,
        grid=(steps,),
        in_specs=[block] * 3
        + [pl.BlockSpec((rows // steps, cols), lambda j: (j, 0))]
        + [held] * len(earlier),
        out_specs=[block] * 3,
        out_shape=[shape] * 3,
        input_output_aliases={4 + k: k for k in range(len(earlier))},
        compiler_params=pltpu.CompilerParams(vmem_limit_bytes=VMEM_LIMIT),
        cost_estimate=pl.CostEstimate(
            flops=20 * rows * cols, bytes_accessed=26 * rows * cols, transcendentals=2 * rows * cols
        ),
        name="adamw",
    )(*state, grad, *earlier)


def adamw_layers(state, grads):
    layers, rows, cols = grads.shape
    steps = 2 if rows % 32 == 0 else 1
    block = pl.BlockSpec((1, rows // steps, cols), lambda k, j: (k, j, 0))
    back = pl.BlockSpec((1, rows // steps, cols), lambda k, j: (layers - 1 - k, j, 0))
    return pl.pallas_call(
        adamw_kernel,
        grid=(layers, steps),
        in_specs=[block] * 3 + [back],
        out_specs=[block] * 3,
        out_shape=[jax.ShapeDtypeStruct(state[0].shape, F32)] * 3,
        compiler_params=pltpu.CompilerParams(vmem_limit_bytes=VMEM_LIMIT),
        cost_estimate=pl.CostEstimate(
            flops=20 * grads.size, bytes_accessed=26 * grads.size, transcendentals=2 * grads.size
        ),
        name="adamw",
    )(*state, grads)


def turned(arrays):
    return tuple(jnp.swapaxes(array, 1, 2) for array in arrays)


def body(
    block_in,
    cotangent,
    positions,
    attend_weight,
    attend_moment,
    attend_variance,
    output_weight,
    output_moment,
    output_variance,
    expand_weight,
    expand_moment,
    expand_variance,
    reduce_weight,
    reduce_moment,
    reduce_variance,
    gains,
    gains_moment,
    gains_variance,
):
    size = lax.axis_size("fsdp")
    cycle = lax.axis_size("ctx")
    row = lax.axis_index("fsdp")
    column = lax.axis_index("ctx")
    model = block_in.shape[2]
    att_rows, att_cols = attend_weight.shape[1:]
    out_rows, out_cols = output_weight.shape[1:]
    exp_rows, exp_cols = expand_weight.shape[1:]
    red_rows, red_cols = reduce_weight.shape[1:]
    chunk = exp_cols // size
    gain_cols = gains.shape[1]
    plane = column // 2
    by_half = attend_pairs(size, cycle)
    holds_values = column >= size + size // 2
    mixed_up = jnp.logical_and(column >= size, row % 2 == 1)
    half = att_cols // 2

    def send_attend(weight):
        low = weight.astype(BF16)
        lead, tail = exchange_attend(
            low[..., :half], low[..., half:], holds_values, mixed_up, by_half[0], by_half[1]
        )
        block = jnp.concatenate([lead, tail], axis=2)
        return jnp.concatenate([block, jnp.swapaxes(output_weight.astype(BF16), 1, 2)], axis=1)

    def exchange_rows(parts):
        return parts_from(exchange(parts_for(parts, row, size), "fsdp", 1, size), row)

    def send_feed(layer, *events):
        expand = expand_weight[layer].astype(BF16).reshape(exp_rows, size, chunk)
        reduce = reduce_weight[layer].astype(BF16).reshape(size, chunk, red_cols)
        parts = [jnp.transpose(expand, (1, 0, 2)), jnp.transpose(reduce, (0, 2, 1))]
        return exchange_rows(after(jnp.concatenate(parts, axis=1), *events))

    def gather(payload):
        return lax.all_gather(payload, "ctx", axis=0, tiled=False)

    pieces = []
    rest = gains
    for _ in range(GAIN_PARTS):
        part = rest.astype(BF16)
        rest = rest - part.astype(F32)
        pieces.append(part)
    gain_own = jnp.stack(pieces)
    gain_all = parts_from(exchange([gain_own] * size, "fsdp", 1, size), row)
    gain_flat = gain_all.reshape(-1, att_cols)
    gain_used = gain_flat.shape[0]

    tokens = block_in.shape[1]
    digits = jnp.stack([positions[0] // RUN, positions[0] % RUN], axis=1).astype(BF16)
    digits = jnp.pad(digits, ((0, 0), (0, LANES - digits.shape[1])))
    both = jnp.concatenate([block_in[0], digits, cotangent[0]], axis=1)
    both = parts_for(both.reshape(size, -1, both.shape[-1]), row, size)
    both, attend_first = lax.optimization_barrier((both, attend_weight))
    both = to_plane_rows(both, size, row)
    stream_low = to_plane(both[..., : model + LANES], size, plane)
    attend_sent = send_attend(attend_first)
    gain_rows = jnp.pad(gain_flat, ((0, GAIN_ROWS - gain_used), (0, 0)))
    payload = jnp.concatenate([attend_sent.reshape(-1, att_cols), gain_rows])
    payload, stream_low = lax.optimization_barrier((payload, stream_low))
    attn_parts = gather(payload)
    payload, both = lax.optimization_barrier((payload, both))
    payload = send_feed(0, payload)
    mlp_parts = [gather(payload)]
    back_low = to_plane(both[..., model + LANES :], size, plane)
    payload, stream_low = lax.optimization_barrier((payload, stream_low))
    stream_all = gather_tokens(stream_low, size)
    order = stream_all[:, model : model + 2].astype(jnp.int32)
    order = order[:, 0] * RUN + order[:, 1]
    order_far = swap_core(order, cycle)
    stream_first = stream_all[:, :model]
    stream_low = stream_low[:, :model]
    payload = send_feed(1, stream_all)
    mlp_parts.append(gather(payload))
    payload, back_low = lax.optimization_barrier((payload, back_low))
    back_all = gather_tokens(back_low, size)
    attn_rows = att_rows + out_cols
    gain_table = attn_parts[:, LAYERS * attn_rows : LAYERS * attn_rows + gain_used]
    gain_table = gain_table.reshape(cycle, size, GAIN_PARTS, 2 * LAYERS, gain_cols).astype(F32)
    gain_table = gain_table[:, :, 0] + gain_table[:, :, 1] + gain_table[:, :, 2]
    gain_table = jnp.transpose(gain_table, (2, 1, 0, 3)).reshape(2 * LAYERS, model)

    def attn_weights(layer):
        part = attn_parts[:, layer * attn_rows : (layer + 1) * attn_rows]
        block = part[:, :att_rows]
        return (
            block[:size].reshape(model, att_cols),
            block[size:].reshape(model, att_cols),
            part[:, att_rows:attn_rows].reshape(model, out_rows),
        )

    freq = THETA ** (-2.0 * jnp.arange(HEAD // 2, dtype=F32) / HEAD)
    angle = freq[:, None] * order.astype(F32)[None, :]
    cosine, sine = (jnp.cos(angle), jnp.sin(angle))

    stream = stream_low.astype(F32)
    stream_first = stream_first.astype(F32)
    saved = []
    for layer in range(LAYERS):
        gain_attend, gain_mix = (gain_table[2 * layer], gain_table[2 * layer + 1])
        query_weight, pair_weight, output_t = attn_weights(layer)
        if layer == 0:
            acts = (stream_first * inverse_rms(stream_first) * gain_attend).astype(BF16)
        else:
            acts = gather_tokens((stream * inverse_rms(stream) * gain_attend).astype(BF16), size)
        queries = rotate(dot(query_weight, acts, 0, 1), cosine, sine).astype(BF16)
        pair = dot(pair_weight, acts, 0, 1)
        pair = jnp.concatenate(
            [rotate(pair[: pair.shape[0] // 2], cosine, sine), pair[pair.shape[0] // 2 :]]
        ).astype(BF16)
        pair_far = swap_core(pair, cycle)
        mixed, totals = attend(queries, pair, pair_far, order, order_far)
        middle = stream + scatter_tokens(dot(mixed, output_t, 0, 1), size)
        middle_low = gather_tokens((middle * inverse_rms(middle) * gain_mix).astype(BF16), size)
        if layer == 0:
            mlp_parts[0] = after(mlp_parts[0], back_all)
        if layer == LAYERS - 1:
            hidden, grad_gate, grad_up, mlp_payload = feed_last(middle_low, back_all, mlp_parts[layer])
            gate, up = (None, None)
        else:
            gate, up, hidden, partial = feed(middle_low, mlp_parts[layer])
        if layer < LAYERS - 1:
            stream_next = middle + scatter_tokens(partial, size)
        saved.append((stream, acts, queries, pair, pair_far, mixed, totals, middle, middle_low, gate, up, hidden))
        stream = stream_next

    back = back_low.astype(F32)
    gain_grads = [None] * (2 * LAYERS)

    def reduce(payload):
        return lax.psum_scatter(payload, "ctx", scatter_dimension=0, tiled=False)

    mlp_grads = {}
    attn_grads = []

    for layer in reversed(range(LAYERS)):
        stream, acts, queries, pair, pair_far, mixed, totals, middle, middle_low, gate, up, hidden = saved[layer]
        gain_attend, gain_mix = (gain_table[2 * layer], gain_table[2 * layer + 1])
        query_weight, pair_weight, output_t = attn_weights(layer)
        if layer < LAYERS - 1:
            back_all = gather_tokens(back.astype(BF16), size)
            grad_gate, grad_up, mlp_payload = feed_turn(
                middle_low, back_all, hidden, gate, up, mlp_parts[layer]
            )
        else:
            last = (middle, hidden)
        mlp_grads[layer] = reduce(mlp_payload)
        grad_gate, mlp_payload = lax.optimization_barrier((grad_gate, mlp_payload))
        specs = block_specs(mlp_parts[layer])
        grad_partial = feed_sum(
            feed_input_kernel, "feed_input", [grad_gate, grad_up], mlp_parts[layer], specs[:2]
        )
        grad_middle = scatter_tokens(grad_partial, size)
        change, gain_grads[2 * layer + 1] = norm_back(middle, gain_mix, grad_middle)
        back = back + change
        back_attend = gather_tokens(back.astype(BF16), size)
        if layer == 0:
            early = after(mlp_grads[1], back_attend)
        grad_mixed = dot(output_t, back_attend, 0, 1).astype(BF16)
        grad_query, key_own, key_far, value_own, value_far = attend_back(
            queries, grad_mixed, pair, pair_far, order, order_far, totals
        )
        from_far = swap_core(jnp.concatenate([key_far, value_far]).astype(BF16), cycle).astype(F32)
        rows_kv = key_own.shape[0]
        grad_key = key_own + from_far[:rows_kv]
        grad_value = value_own + from_far[rows_kv:]
        grad_query = rotate(grad_query.astype(BF16).astype(F32), cosine, -sine).astype(BF16)
        grad_key = rotate(grad_key.astype(BF16).astype(F32), cosine, -sine).astype(BF16)
        grad_pair = jnp.concatenate([grad_key, grad_value.astype(BF16)])
        grad_acts = dot(grad_query, query_weight, 0, 1) + dot(grad_pair, pair_weight, 0, 1)
        parts = [
            jnp.concatenate([dot(acts, grad_query, 0, 1), dot(acts, grad_pair, 0, 1)])
            .astype(BF16)
            .reshape(cycle, att_rows, att_cols),
            dot(back_attend, mixed, 0, 1).astype(BF16).reshape(cycle, out_cols, out_rows),
        ]
        grad_stream = scatter_tokens(grad_acts, size)
        change, gain_grads[2 * layer] = norm_back(stream, gain_attend, grad_stream)
        back = back + change
        if layer == 0:
            gain_grads[0] = jnp.sum(grad_acts * stream_first * inverse_rms(stream_first), axis=0)
            table = jnp.stack(gain_grads).reshape(2 * LAYERS, size, cycle, gain_cols)
            table = jnp.transpose(table, (1, 2, 0, 3)).reshape(size, cycle, -1)
            table = sum(exchange(parts_for(table, row, size), "fsdp", 1, size))
            table = jnp.pad(table, ((0, 0), (0, att_cols - table.shape[1]))).astype(BF16)
            parts.append(jnp.pad(table[:, None], ((0, 0), (0, GAIN_ROWS - 1), (0, 0))))
        attn_payload = jnp.concatenate(parts, axis=1)
        if layer > 0:
            attn_payload, back = lax.optimization_barrier((attn_payload, back))
        attn_grads.append(reduce(attn_payload))

    states = {
        "attend": (attend_weight, attend_moment, attend_variance),
        "output": turned((output_weight, output_moment, output_variance)),
        "expand": (expand_weight, expand_moment, expand_variance),
        "reduce": turned((reduce_weight, reduce_moment, reduce_variance)),
    }
    renewed = {name: () for name in states}

    def renew(name, layer, grad):
        renewed[name] = adamw_layer(states[name], grad, layer, renewed[name])

    def renew_feed(layer, mlp_grad):
        expand = jnp.transpose(mlp_grad[:, :exp_rows], (1, 0, 2)).reshape(exp_rows, exp_cols)
        reduce = jnp.transpose(mlp_grad[:, exp_rows:], (1, 0, 2)).reshape(red_cols, red_rows)
        renew("expand", layer, expand)
        renew("reduce", layer, reduce)

    def renew_attend(attn_grads):
        block = jnp.stack([grad[:att_rows] for grad in attn_grads])
        lead, tail = exchange_attend(
            block[..., :half],
            block[..., half:],
            mixed_up,
            holds_values,
            backwards(by_half[0]),
            backwards(by_half[1]),
        )
        output = jnp.stack([grad[att_rows:attn_rows] for grad in attn_grads])
        renewed["output"] = adamw_layers(states["output"], output)
        renewed["attend"] = adamw_layers(states["attend"], jnp.concatenate([lead, tail], axis=2))

    sent_last = exchange_rows(early)
    block_out = feed_sum(
        feed_out_kernel, "feed_out", [after(last[1], attn_payload)], mlp_parts[-1], specs[2:]
    )
    block_out = last[0] + scatter_tokens(block_out, size)
    mlp_grads[0], sent_last, block_out = lax.optimization_barrier(
        (mlp_grads[0], sent_last, block_out)
    )
    sent = exchange_rows(mlp_grads[0])
    outs = from_plane(jnp.concatenate([block_out, back], axis=1).astype(BF16), size)
    attn_grads[-1], outs, sent = lax.optimization_barrier((attn_grads[-1], outs, sent))
    renew_attend(attn_grads)
    renew_feed(1, sent_last)
    renew_feed(0, sent)
    outs = from_plane_rows(outs, size, row, plane)
    grad_gains = attn_grads[-1][attn_rows, : 2 * LAYERS * gain_cols]
    grad_gains = grad_gains.astype(F32).reshape(2 * LAYERS, gain_cols)
    for name in ("output", "reduce"):
        renewed[name] = turned(renewed[name])
    results = [value for name in states for value in renewed[name]]
    results += list(adamw(gains, gains_moment, gains_variance, grad_gains, RATE_GAIN, 0.0))
    outs = outs.astype(F32)
    return (outs[None, :, :model], outs[None, :, model:], *results)


def solution(mesh):
    tokens = P("fsdp", "ctx", None)
    matrix = P(None, "fsdp", "ctx")
    gain = P(None, ("fsdp", "ctx"))
    return jax.shard_map(
        body,
        mesh=mesh,
        in_specs=(tokens, tokens, P("fsdp", "ctx")) + (matrix,) * 12 + (gain,) * 3,
        out_specs=(tokens, tokens) + (matrix,) * 12 + (gain,) * 3,
        check_vma=False,
    )
```
